256 devices in a mesh: section: 8 (over x, core), dp: 32 (over z, y).
Axes of the slice: x: 4, y: 4, z: 8, core: 2. Of those that a mesh axis runs over, the one named last changes fastest.
Arguments:
- layer_inputs: bfloat16 [8, 5120, 8192], P('section', 'dp'), may hold values from -460 to 460
- queries: bfloat16 [8, 5120, 8192], P('section', 'dp'), may hold values from -9 to 9
- keys: bfloat16 [8, 5120, 512], P('section', 'dp'), may hold values from -4.5 to 4.5
- gains: bfloat16 [8, 8192], P('section'), may hold values from 0.4 to 47
- value_weights: bfloat16 [8, 8192, 512], P('section', 'dp'), may hold values from -0.05634757 to 0.05634757
- out_grad: bfloat16 [5120, 8192], P('dp', 'section'), may hold values from -0.04332382 to 0.04332382
Outputs:
- value_grads: float32 [8, 8192, 512], P('section', 'dp')
The draws below stay inside these ranges and needn't reach their ends.
All inputs are finite; a program needn't handle non-finite values.
Results may differ from the reference program's by a relative error of at most 0.03.
Values may be sent and summed in bfloat16 or wider, within the bound.
A program may use at most 192 MiB of HBM per device.

```python
import math
import jax
import jax.numpy as jnp
from jax import lax

QH = 64
KVH = 4
HD = 128
MB_TOK = 80
D = 8192
SECTIONS = 8
TOK_DEV = 160
TOKENS = 5120
N_DP = 32


def shared_signs(key):
    feature_signs = jax.random.rademacher(jax.random.fold_in(key, 211), (SECTIONS, D), jnp.float32)
    value_signs = jax.random.rademacher(jax.random.fold_in(key, 213), (SECTIONS, KVH * HD), jnp.float32)
    return (feature_signs, value_signs)


def draw_queries(key, part):
    key = jax.random.fold_in(key, 3)
    extent = (SECTIONS, TOKENS, KVH, QH // KVH, HD)
    sample = jnp.clip(jax.random.normal(key, extent, jnp.float32), -4.0, 4.0)
    return sample.reshape(SECTIONS, TOKENS, QH * HD).astype(jnp.bfloat16)


def draw_keys(key, part):
    key = jax.random.fold_in(key, 5)
    extent = (SECTIONS, TOKENS, KVH, HD)
    sample = jnp.clip(jax.random.normal(key, extent, jnp.float32), -4.0, 4.0)
    return sample.reshape(SECTIONS, TOKENS, KVH * HD).astype(jnp.bfloat16)


def draw_layer_inputs(key, part):
    feature_signs, _ = shared_signs(key)
    key = jax.random.fold_in(key, 7)
    first_key, second_key, third_key, fourth_key = jax.random.split(key, 4)
    extent = (SECTIONS, TOKENS, D)
    sample = jnp.clip(jax.random.normal(first_key, extent, jnp.float32), -4.0, 4.0)
    spread = math.log(10.0)
    lowest = 0.3
    offset = 0.2
    token_signs = jax.random.rademacher(fourth_key, (SECTIONS, TOKENS, 1), jnp.float32)
    sample = sample + (offset + token_signs) * feature_signs[:, None, :]
    column_scale = jnp.exp(jax.random.uniform(second_key, (1, 1, D), jnp.float32, 0.0, spread))
    row_scale = lowest * jnp.exp(jax.random.uniform(third_key, (SECTIONS, TOKENS, 1), jnp.float32, 0.0, spread))
    return (sample * column_scale * row_scale).astype(jnp.bfloat16)


def draw_gains(key, part):
    key = jax.random.fold_in(key, 9)
    section_place = jnp.arange(SECTIONS, dtype=jnp.float32)[:, None] / max(SECTIONS - 1, 1)
    feature_place = jnp.arange(D, dtype=jnp.float32)[None, :] / (D - 1)
    sample = 1.0 + 0.15 * jnp.clip(jax.random.normal(key, (SECTIONS, D), jnp.float32), -4.0, 4.0)
    growth = 4.0
    return (sample * growth ** section_place * growth ** feature_place).astype(jnp.bfloat16)


def draw_value_weights(key, part):
    feature_signs, value_signs = shared_signs(key)
    key = jax.random.fold_in(key, 13)
    extent = (SECTIONS, D, KVH * HD)
    sample = jnp.clip(jax.random.normal(key, extent, jnp.float32), -4.0, 4.0)
    sample = sample + feature_signs[:, :, None] * value_signs[:, None, :]
    return (sample * (1.0 / math.sqrt(D))).astype(jnp.bfloat16)


def draw_out_grad(key, part):
    key = jax.random.fold_in(key, 11)
    first_key, second_key = jax.random.split(key)
    extent = (TOKENS, D)
    shift_draw = jnp.clip(jax.random.normal(second_key, (1, D), jnp.float32), -4.0, 4.0)
    sample = jnp.clip(jax.random.normal(first_key, extent, jnp.float32), -3.5, 3.5)
    sample = (sample + 0.06 * shift_draw) * (0.8 / math.sqrt(TOKENS))
    return sample.astype(jnp.bfloat16)


def setup_inputs(seed: int = 0) -> dict:
    key_of = jax.random.split(jax.random.key(seed), 7)
    return {
        "layer_inputs": draw_layer_inputs(jax.random.fold_in(key_of[6], 71), 0),
        "queries": draw_queries(jax.random.fold_in(key_of[6], 71), 0),
        "keys": draw_keys(jax.random.fold_in(key_of[6], 71), 0),
        "gains": draw_gains(jax.random.fold_in(key_of[6], 71), 0),
        "value_weights": draw_value_weights(jax.random.fold_in(key_of[6], 71), 0),
        "out_grad": draw_out_grad(jax.random.fold_in(key_of[6], 71), 0),
    }


EPSILON = 1e-05

def section_pass(layer_in, query_in, key_in, gain, value_weight, upstream):
    sequences = TOKENS // MB_TOK
    per_group = QH // KVH
    floats = layer_in.astype(jnp.float32)
    inverse = lax.rsqrt(lax.optimization_barrier(jnp.mean(floats * floats, axis=-1, keepdims=True)) + EPSILON)
    normed = floats * inverse
    gain_rows = gain.astype(jnp.float32)
    hidden = (normed * gain_rows).astype(jnp.bfloat16)
    query_rows = query_in.astype(jnp.float32).reshape(sequences, MB_TOK, KVH, per_group, HD)
    key_rows = key_in.astype(jnp.float32).reshape(sequences, MB_TOK, KVH, HD)
    scores = jnp.einsum('btgqd,bsgd->bgqts', query_rows, key_rows) * HD ** (-0.5)
    causal = jnp.arange(MB_TOK)[:, None] >= jnp.arange(MB_TOK)[None, :]
    scores = jnp.where(causal, scores, -jnp.inf)
    row_max = lax.optimization_barrier(jnp.max(scores, axis=-1, keepdims=True))
    exponent = jnp.exp(scores - row_max)
    probabilities = (exponent / lax.optimization_barrier(jnp.sum(exponent, axis=-1, keepdims=True))).astype(jnp.bfloat16)
    upstream_heads = upstream.astype(jnp.float32).reshape(sequences, MB_TOK, KVH, per_group, HD)
    value_grad = jnp.einsum('bgqts,btgqd->bsgd', probabilities.astype(jnp.float32), upstream_heads)
    value_grad = value_grad.reshape(TOKENS, KVH * HD).astype(jnp.bfloat16)
    hidden_grad = lax.dot_general(value_grad, value_weight, (((1,), (1,)), ((), ())), preferred_element_type=jnp.float32)
    scaled = hidden_grad * gain_rows
    inner_mean = lax.optimization_barrier(jnp.mean(scaled * normed, axis=-1, keepdims=True))
    outgoing = (upstream.astype(jnp.float32) + inverse * (scaled - normed * inner_mean)).astype(jnp.bfloat16)
    return (hidden, value_grad, outgoing)

def replica_sum(hidden, value_grad):
    hidden_blocks = hidden.reshape(N_DP, TOK_DEV, D)
    grad_blocks = value_grad.reshape(N_DP, TOK_DEV, KVH * HD)

    def accumulate(running, blocks_pair):
        partial_value = jnp.dot(blocks_pair[0].T, blocks_pair[1], preferred_element_type=jnp.float32)
        partial_value = lax.optimization_barrier(partial_value.astype(jnp.bfloat16)).astype(jnp.float32)
        return (running + partial_value, None)
    running, _ = lax.scan(accumulate, jnp.zeros((D, KVH * HD), jnp.float32), (hidden_blocks, grad_blocks))
    return running

def reference(layer_inputs, queries, keys, gains, value_weights, out_grad):
    upstream = out_grad
    section_grads = []
    for layer_index in reversed(range(SECTIONS)):
        hidden, value_grad, upstream = section_pass(layer_inputs[layer_index], queries[layer_index], keys[layer_index], gains[layer_index], value_weights[layer_index], upstream)
        section_grads.append(replica_sum(hidden, value_grad))
    weight_sum = jnp.stack(section_grads[::-1])
    total_norm = jnp.sqrt(jnp.sum(weight_sum * weight_sum))
    factor = jnp.minimum(1.0, math.sqrt(SECTIONS * D * KVH * HD) / total_norm)
    return weight_sum * factor
```

```python
import jax
import jax.numpy as jnp
from jax import lax
from jax.experimental import pallas as pl
from jax.experimental.pallas import tpu as pltpu
from jax.sharding import PartitionSpec as P

MESH = pl.DeviceIdType.MESH
F32, BF16 = jnp.float32, jnp.bfloat16
QH, KVH, HD, SEQ, D = 64, 4, 128, 80, 8192
PER = QH // KVH
GROUP = PER * HD
KV = KVH * HD
STACK = PER * SEQ
BLK = 256
LAYERS, NX, NY, NZ = 8, 4, 4, 8
EPSILON = 1e-05
NT = (((1,), (1,)), ((), ()))


def mod(a, n):
    return lax.rem(a + 2 * n, n)


def aligned(index, size):
    return pl.multiple_of(index * size, size)


def body(
    x_hbm, q_hbm, k_ref, gain_ref, w_hbm, og_hbm, out_ref,
    xv, qv, wall, xi, pt, inv_in, gain_in, p_own, inv_own, mask, top, up, vgb, vr,
    h_own, h_all, vg_all, vg_t, rs_send, rs_recv, total, n_own, n1, n2, n3,
    s_loc, s_x, r_x, s_p, r_p, s_i, r_i, s_g, r_g, s_og, r_og, s_wx, r_w, s_z, s_y, s_yf, r_y,
    s_pt, r_pt, s_v, r_v, s_vg, r_vg, s_vp, r_vp, s_vy, r_vy, s_h, r_h, s_rs, r_rs, s_n, r_n,
):
    sec, dp = lax.axis_index("section"), lax.axis_index("dp")
    x, c = lax.div(sec, 2), lax.rem(sec, 2)
    z, y = lax.div(dp, NY), lax.rem(dp, NY)
    mate = sec + 1 - 2 * c

    def at_dp(zz, yy):
        return zz * NY + yy

    def send(src, dst, ssem, rsem, section=sec, replica=dp):
        return pltpu.make_async_remote_copy(
            src_ref=src, dst_ref=dst, send_sem=ssem, recv_sem=rsem,
            device_id={"section": section, "dp": replica}, device_id_type=MESH,
        )

    def arrived(dst, rsem):
        send(dst, dst, s_loc.at[7], rsem, section=mate).wait_recv()

    pending = []

    def go(copy, when=None):
        if when is None:
            copy.start()
        else:
            pl.when(when)(copy.start)
        pending.append((copy, when))

    barrier = pltpu.get_barrier_semaphore()
    friends = [(mod(sec + k, LAYERS), dp) for k in range(1, LAYERS)]
    friends += [(sec, at_dp(z, mod(y + k, NY))) for k in range(1, NY)]
    friends += [(sec, at_dp(mod(z + k, NZ), y)) for k in range(1, NZ)]
    for section, replica in friends:
        pl.semaphore_signal(
            barrier, inc=1, device_id={"section": section, "dp": replica}, device_id_type=MESH
        )
    pl.semaphore_wait(barrier, len(friends))

    w_home = lax.div(z, 2)
    w_zl = lax.rem(z, 2)
    w_away = w_home != x
    go(
        send(
            w_hbm, wall.at[c, x, w_zl * NY + y], s_wx, r_w.at[x, w_zl], section=2 * w_home + c
        ),
        w_away,
    )
    w_local = pltpu.make_async_copy(w_hbm, wall.at[c, x, w_zl * NY + y], s_loc.at[0])
    pl.when(jnp.logical_not(w_away))(w_local.start)
    x_load = pltpu.make_async_copy(x_hbm, xv, s_loc.at[1])
    q_load = pltpu.make_async_copy(q_hbm, qv, s_loc.at[2])
    q_load.start()
    x_load.start()

    def rows(b):
        return pl.ds(pl.multiple_of(b * SEQ, 16), SEQ)

    half = D // LAYERS
    go(
        send(
            og_hbm.at[rows(1 - c)], top.at[:, pl.ds(aligned(c, half), half)], s_og, r_og,
            section=mate,
        )
    )
    og_local = pltpu.make_async_copy(
        og_hbm.at[rows(c)], top.at[:, pl.ds(aligned(c, half), half)], s_loc.at[3]
    )
    og_local.start()

    def dest(k):
        section = mod(sec + k, LAYERS)
        return section, lax.div(section, 2), lax.rem(section, 2)

    def block(ref, b, g):
        return ref.at[rows(b), pl.ds(aligned(g, GROUP), GROUP)]

    for k in range(1, LAYERS):
        section, g, b = dest(k)
        go(send(block(x_hbm, b, g), xi.at[sec], s_x.at[k], r_x.at[sec], section=section))
        go(
            send(
                gain_ref.at[:, pl.ds(aligned(g, GROUP), GROUP)], gain_in.at[sec], s_g.at[k],
                r_g.at[sec], section=section,
            )
        )
    xi_local = pltpu.make_async_copy(block(x_hbm, c, x), xi.at[sec], s_loc.at[4])
    xi_local.start()
    gain_in[sec] = gain_ref[:, pl.ds(aligned(x, GROUP), GROUP)]

    key_row = lax.broadcasted_iota(jnp.int32, (SEQ, STACK), 0)
    query_row = lax.rem(lax.broadcasted_iota(jnp.int32, (SEQ, STACK), 1), SEQ)
    mask[...] = jnp.where(key_row <= query_row, 0.0, -1e30).astype(F32)
    q_load.wait()

    def probabilities(g, b):
        keys = k_ref[rows(b), pl.ds(aligned(g, HD), HD)]
        stacked = jnp.concatenate(
            [
                qv[rows(b), pl.ds(pl.multiple_of(g * GROUP + h * HD, HD), HD)]
                for h in range(PER)
            ],
            axis=0,
        )
        scores = lax.dot_general(keys, stacked, NT, preferred_element_type=F32)
        scores = scores * HD ** (-0.5) + mask[...]
        exponent = jnp.exp(scores - jnp.max(scores, axis=0, keepdims=True))
        return (exponent / jnp.sum(exponent, axis=0, keepdims=True)).astype(BF16)

    def p_copy(k):
        section, g, b = dest(k)
        return send(p_own.at[k], pt.at[sec], s_p.at[k], r_p.at[sec], section=section)

    @pl.loop(1, LAYERS)
    def _(k):
        section, g, b = dest(k)
        p_own[k] = probabilities(g, b)
        p_copy(k).start()

    pt[sec] = probabilities(x, c)

    x_load.wait()

    def squares(i, acc):
        v = xv[:, pl.ds(aligned(i, HD), HD)].astype(F32)
        return acc + v * v

    acc = lax.fori_loop(0, D // HD, squares, jnp.zeros((2 * SEQ, HD), F32))
    mean = jnp.sum(acc, axis=1, keepdims=True) * (1.0 / D)
    inv_own[...] = jnp.broadcast_to(lax.rsqrt(mean + EPSILON), (2 * SEQ, HD))
    for k in range(1, LAYERS):
        section, g, b = dest(k)
        go(send(inv_own.at[rows(b)], inv_in.at[sec], s_i.at[k], r_i.at[sec], section=section))
    inv_in[sec] = inv_own[rows(c)]

    @pl.loop(0, D // BLK)
    def _(i):
        cols = pl.ds(aligned(i, BLK), BLK)
        normed = xv[:, cols].astype(F32) * inv_own[:, 0:1]
        h_own[lax.rem(i, NY), :, pl.ds(aligned(lax.div(i, NY), BLK), BLK)] = (
            normed * gain_ref[0:1, cols]
        ).astype(BF16)

    d = mod(2 * x - z, NZ)
    downward = d <= 3
    step = jnp.where(downward, -1, 1)
    first = jnp.where(downward, 0, 1)
    source = jnp.logical_or(d == 0, d == 7)
    onward = jnp.logical_and(d != 3, d != 4)
    z_out, z_in = mod(z + step, NZ), mod(z - step, NZ)
    y_right, y_left, y_far = mod(y + 1, NY), mod(y - 1, NY), mod(y + 2, NY)

    def piece_ref(u, piece, yy):
        return wall.at[c, u, piece * NY + yy]

    def column(u):
        for o in range(2):
            piece = first if o == 0 else 1 - first
            ref = piece_ref(u, piece, y)
            sem = r_w.at[u, piece]
            if o == 0:
                mine = jnp.logical_and(source, x == u)
                pl.when(mine)(w_local.wait)
                pl.when(jnp.logical_not(mine))(lambda ref=ref, sem=sem: arrived(ref, sem))
                go(send(ref, ref, s_z.at[u, 2], sem, replica=at_dp(z_in, y)), source)
            else:
                arrived(ref, sem)
            go(send(ref, ref, s_z.at[u, o], sem, replica=at_dp(z_out, y)), onward)
            for i, yy in enumerate((y_right, y_left)):
                go(send(ref, ref, s_y.at[u, o, i], r_y.at[u, piece, y], replica=at_dp(z, yy)))

    def row(u):
        def near(piece, yy):
            arrived(piece_ref(u, piece, yy), r_y.at[u, piece, yy])

        def forward(piece, source_y, to_y, i):
            ref = piece_ref(u, piece, source_y)
            go(send(ref, ref, s_yf.at[u, i], r_y.at[u, piece, source_y], replica=at_dp(z, to_y)))

        near(0, y_left)
        forward(0, y_left, y_right, 0)
        near(1, y_right)
        forward(1, y_right, y_left, 1)
        near(1, y_left)
        near(0, y_right)

    def finish(u):
        for piece in range(2):
            arrived(piece_ref(u, piece, y_far), r_y.at[u, piece, y_far])
        go(send(wall.at[c, u], wall.at[c, u], s_pt.at[u], r_pt.at[u], section=mate))

    def weights_ready(u):
        arrived(wall.at[1 - c, u], r_pt.at[u])

    column(3)
    column(2)
    row(3)
    column(1)
    row(2)
    finish(3)
    column(0)
    row(1)
    finish(2)
    row(0)
    finish(1)
    finish(0)

    for k in range(1, NY):
        yy = mod(y + k, NY)
        mine = h_all.at[pl.ds(aligned(y, 2 * SEQ), 2 * SEQ)]
        go(send(h_own.at[yy], mine, s_h.at[k], r_h.at[y], replica=at_dp(z, yy)))
    h_all[pl.ds(aligned(y, 2 * SEQ), 2 * SEQ), :] = h_own[y]

    og_local.wait()
    arrived(top.at[:, pl.ds(aligned(1 - c, half), half)], r_og)
    for h in range(PER):
        up[h * SEQ:(h + 1) * SEQ, :] = top[:, h * HD:(h + 1) * HD]
    xi_local.wait()
    for u in range(NX):
        weights_ready(u)
    for k in range(1, LAYERS):
        section = mod(sec + k, LAYERS)
        arrived(xi.at[section], r_x.at[section])
        arrived(pt.at[section], r_p.at[section])
        arrived(inv_in.at[section], r_i.at[section])
        arrived(gain_in.at[section], r_g.at[section])

    def peers():
        return [mod(x + k, NX) for k in range(1, NX)]

    def w_block(s, i):
        return wall[lax.rem(s, 2), lax.div(s, 2), i]

    def v_copies(s):
        return [
            send(vr.at[s, x], vr.at[s, x], s_v.at[s, k], r_v.at[s, x], section=2 * g + c)
            for k, g in enumerate(peers())
        ]

    def projected(s):
        inverse = inv_in[s][:, 0:1]
        acc = jnp.zeros((SEQ, KV), F32)
        for i in range(GROUP // BLK):
            cols = slice(i * BLK, (i + 1) * BLK)
            normed = xi[s, :, cols].astype(F32) * inverse
            hidden = (normed * gain_in[s, 0:1, cols]).astype(BF16)
            acc += jnp.dot(hidden, w_block(s, i), preferred_element_type=F32)
        vr[s, x] = acc.astype(BF16)
        for copy in v_copies(s):
            copy.start()

    @pl.loop(0, LAYERS)
    def _(t):
        projected(LAYERS - 1 - t)

    def vg_cols(s, g):
        return vgb.at[s, :, pl.ds(aligned(g, HD), HD)]

    def vg_copies(s):
        return [
            send(vg_cols(s, x), vg_cols(s, x), s_vg.at[s, k], r_vg.at[s, x], section=2 * g + c)
            for k, g in enumerate(peers())
        ]

    def vp_copy(s):
        place = vg_all.at[pl.ds(pl.multiple_of(y * 2 * SEQ + c * SEQ, 16), SEQ)]
        return send(vgb.at[s], place, s_vp, r_vp, section=mate)

    def value_grad(s):
        grad = jnp.dot(pt[s], up[...], preferred_element_type=F32).astype(BF16)
        vgb[s, :, pl.ds(aligned(x, HD), HD)] = grad
        for copy in vg_copies(s):
            copy.start()
        for g in peers():
            arrived(vr.at[s, g], r_v.at[s, g])
        for g in peers():
            arrived(vg_cols(s, g), r_vg.at[s, g])
        pl.when(s == mate)(lambda: vp_copy(s).start())

    def layer(s):
        value_grad(s)
        grads = vgb[s]
        inner = sum(vr[s, g].astype(F32) for g in range(NX))
        inner = jnp.sum(grads.astype(F32) * inner, axis=1, keepdims=True) * (1.0 / D)
        inverse = inv_in[s][:, 0:1]
        for i in range(GROUP // BLK):
            cols = slice(i * BLK, (i + 1) * BLK)
            hidden_grad = lax.dot_general(grads, w_block(s, i), NT, preferred_element_type=F32)
            normed = xi[s, :, cols].astype(F32) * inverse
            change = inverse * (hidden_grad * gain_in[s, 0:1, cols] - normed * inner)
            for j in range(BLK // HD):
                h = i * (BLK // HD) + j
                place = slice(h * SEQ, (h + 1) * SEQ)
                up[place, :] = (
                    up[place, :].astype(F32) + change[:, j * HD:(j + 1) * HD]
                ).astype(BF16)

    @pl.loop(0, LAYERS - 1)
    def _(t):
        layer(LAYERS - 1 - t)

    value_grad(0)

    vg_all[pl.ds(pl.multiple_of(y * 2 * SEQ + c * SEQ, 16), SEQ)] = vgb[sec]
    arrived(vg_all.at[pl.ds(pl.multiple_of(y * 2 * SEQ + (1 - c) * SEQ, 16), SEQ)], r_vp)

    def vg_rows(yy):
        return vg_all.at[pl.ds(aligned(yy, 2 * SEQ), 2 * SEQ)]

    for k in range(1, NY):
        yy = mod(y + k, NY)
        go(send(vg_rows(y), vg_rows(y), s_vy.at[k], r_vy.at[y], replica=at_dp(z, yy)))
    for k in range(1, NY):
        yy = mod(y + k, NY)
        arrived(h_all.at[pl.ds(aligned(yy, 2 * SEQ), 2 * SEQ)], r_h.at[yy])
    for k in range(1, NY):
        yy = mod(y + k, NY)
        arrived(vg_rows(yy), r_vy.at[yy])
    vg_t[...] = vg_all[...].astype(F32).T.astype(BF16)

    def product(way, owner):
        return jnp.dot(
            vg_t[way * BLK:(way + 1) * BLK, :], h_all[:, pl.ds(aligned(owner, BLK), BLK)],
            preferred_element_type=F32,
        )

    def rs_copy(way, k):
        zz = mod(z + 1, NZ) if way == 0 else mod(z - 1, NZ)
        return send(
            rs_send.at[way, k], rs_recv.at[way, k], s_rs.at[way, k], r_rs.at[way, k],
            replica=at_dp(zz, y),
        )

    def owner_at(way, k):
        return mod(z - 1 - k, NZ) if way == 0 else mod(z + 1 + k, NZ)

    for way in range(2):
        rs_send[way, 0] = product(way, owner_at(way, 0)).astype(BF16)
        rs_copy(way, 0).start()

    @pl.loop(1, NZ - 1)
    def _(k):
        for way in range(2):
            total[way] = product(way, owner_at(way, k))
        for way in range(2):
            rs_copy(way, k - 1).wait_recv()
            rs_send[way, k] = (total[way] + rs_recv[way, k - 1].astype(F32)).astype(BF16)
            rs_copy(way, k).start()

    squares_sum = jnp.zeros((1, 1), F32)
    for way in range(2):
        total[way] = product(way, z)
    for way in range(2):
        rs_copy(way, NZ - 2).wait_recv()
        owned = total[way] + rs_recv[way, NZ - 2].astype(F32)
        total[way] = owned
        part = jnp.sum(owned * owned, axis=1, keepdims=True)
        squares_sum += jnp.sum(part, axis=0, keepdims=True)

    stages = (
        (n1, LAYERS, sec, lambda i: (i, dp)),
        (n2, NY, y, lambda i: (sec, at_dp(z, i))),
        (n3, NZ, z, lambda i: (sec, at_dp(i, y))),
    )
    value = jnp.broadcast_to(squares_sum, (8, 128))
    for t, (slots, count, me, place) in enumerate(stages):
        slots[me] = value
        for k in range(1, count):
            section, replica = place(mod(me + k, count))
            go(
                send(
                    slots.at[me], slots.at[me], s_n.at[t, k], r_n.at[t, me], section=section,
                    replica=replica,
                )
            )
        for k in range(1, count):
            i = mod(me + k, count)
            arrived(slots.at[i], r_n.at[t, i])
        value = sum(slots[i] for i in range(count))
    ceiling = float(LAYERS * D * KV) ** 0.5
    factor = jnp.minimum(1.0, ceiling / jnp.sqrt(value[0:1, 0:1]))
    for way in range(2):
        out_ref[:, way * BLK:(way + 1) * BLK] = (total[way] * factor).T

    @pl.loop(1, LAYERS)
    def _(k):
        p_copy(k).wait_send()

    @pl.loop(0, LAYERS)
    def _(s):
        for copy in v_copies(s) + vg_copies(s):
            copy.wait_send()

    vp_copy(mate).wait_send()

    @pl.loop(0, NZ - 1)
    def _(k):
        for way in range(2):
            rs_copy(way, k).wait_send()

    for copy, when in pending:
        if when is None:
            copy.wait_send()
        else:
            pl.when(when)(copy.wait_send)


def shards(layer_inputs, queries, keys, gains, value_weights, out_grad):
    gain_rows = jnp.broadcast_to(gains.astype(F32), (8, D))
    dma, vmem = pltpu.SemaphoreType.DMA, pltpu.VMEM
    scratch = [
        vmem((2 * SEQ, D), BF16),
        vmem((2 * SEQ, D), BF16),
        vmem((2, NX, 2 * NY, BLK, KV), BF16),
        vmem((LAYERS, SEQ, GROUP), BF16),
        vmem((LAYERS, SEQ, STACK), BF16),
        vmem((LAYERS, SEQ, HD), F32),
        vmem((LAYERS, 8, GROUP), F32),
        vmem((LAYERS, SEQ, STACK), BF16),
        vmem((2 * SEQ, HD), F32),
        vmem((SEQ, STACK), F32),
        vmem((SEQ, GROUP), BF16),
        vmem((STACK, HD), BF16),
        vmem((LAYERS, SEQ, KV), BF16),
        vmem((LAYERS, NX, SEQ, KV), BF16),
        vmem((NY, 2 * SEQ, GROUP), BF16),
        vmem((NY * 2 * SEQ, GROUP), BF16),
        vmem((NY * 2 * SEQ, KV), BF16),
        vmem((KV, NY * 2 * SEQ), BF16),
        vmem((2, NZ - 1, BLK, BLK), BF16),
        vmem((2, NZ - 1, BLK, BLK), BF16),
        vmem((2, BLK, BLK), F32),
        vmem((8, 128), F32),
        vmem((LAYERS, 8, 128), F32),
        vmem((NY, 8, 128), F32),
        vmem((NZ, 8, 128), F32),
        dma((8,)),
        dma((LAYERS,)), dma((LAYERS,)),
        dma((LAYERS,)), dma((LAYERS,)),
        dma((LAYERS,)), dma((LAYERS,)),
        dma((LAYERS,)), dma((LAYERS,)),
        dma, dma,
        dma, dma((NX, 2)), dma((NX, 3)), dma((NX, 2, 2)), dma((NX, 2)), dma((NX, 2, NY)),
        dma((NX,)), dma((NX,)),
        dma((LAYERS, NX)), dma((LAYERS, NX)),
        dma((LAYERS, NX)), dma((LAYERS, NX)),
        dma, dma,
        dma((NY,)), dma((NY,)),
        dma((NY,)), dma((NY,)),
        dma((2, NZ)), dma((2, NZ)),
        dma((3, LAYERS)), dma((3, LAYERS)),
    ]
    hbm, whole = pl.BlockSpec(memory_space=pl.ANY), pl.BlockSpec(memory_space=pltpu.VMEM)
    out = pl.pallas_call(
        body,
        out_shape=jax.ShapeDtypeStruct((BLK, KV), F32),
        in_specs=[hbm, hbm, whole, whole, hbm, hbm],
        out_specs=whole,
        scratch_shapes=scratch,
        compiler_params=pltpu.CompilerParams(
            collective_id=0, has_side_effects=True, vmem_limit_bytes=60 * 1024 * 1024
        ),
    )(layer_inputs[0], queries[0], keys[0], gain_rows, value_weights[0], out_grad)
    return out[None]


def solution(mesh):
    return jax.shard_map(
        shards,
        mesh=mesh,
        in_specs=(
            P("section", "dp", None),
            P("section", "dp", None),
            P("section", "dp", None),
            P("section", None),
            P("section", "dp", None),
            P("dp", "section"),
        ),
        out_specs=P("section", "dp", None),
        check_vma=False,
    )
```

```python
import jax
import jax.numpy as jnp
from jax import lax
from jax.experimental import pallas as pl
from jax.experimental.pallas import tpu as pltpu
from jax.sharding import PartitionSpec as P

MESH = pl.DeviceIdType.MESH
F32, BF16 = jnp.float32, jnp.bfloat16
QH, KVH, HD, SEQ, D = 64, 4, 128, 80, 8192
PER = QH // KVH
GROUP = PER * HD
KV = KVH * HD
STACK = PER * SEQ
BLK = 256
CUT = 128
HOPS = 4
STREAMS = KV // CUT
LAYERS, NX, NY, NZ = 8, 4, 4, 8
EPSILON = 1e-05
NT = (((1,), (1,)), ((), ()))


def mod(a, n):
    return lax.rem(a + 2 * n, n)


def aligned(index, size):
    return pl.multiple_of(index * size, size)


def body(
    x_hbm, q_hbm, k_ref, gain_bf, w_hbm, og_hbm, out_ref, gain_ref,
    xv, qv, wall, xi, pt, inv_in, gain_in, p_own, inv_own, mask, top, up, vgb, v_own, v_in, v_all, hg, inner_in,
    h_own, h_all, vg_all, vg_t, rs_send, rs_recv, total, n1, n2, n3,
    s_loc, s_x, r_x, s_p, r_p, s_i, r_i, s_g, r_g, s_og, r_og, s_wx, r_w, s_z, s_y, s_yf, r_y,
    s_pt, r_pt, s_v, r_v, s_w, r_vs, s_in, r_in, s_vg, r_vg, s_vp, r_vp, s_vy, r_vy, s_h, r_h, s_rs, r_rs, s_n, r_n,
):
    sec, dp = lax.axis_index("section"), lax.axis_index("dp")
    x, c = lax.div(sec, 2), lax.rem(sec, 2)
    z, y = lax.div(dp, NY), lax.rem(dp, NY)
    mate = sec + 1 - 2 * c

    def at_dp(zz, yy):
        return zz * NY + yy

    def send(src, dst, ssem, rsem, section=sec, replica=dp):
        return pltpu.make_async_remote_copy(
            src_ref=src, dst_ref=dst, send_sem=ssem, recv_sem=rsem,
            device_id={"section": section, "dp": replica}, device_id_type=MESH,
        )

    def arrived(dst, rsem):
        send(dst, dst, s_loc.at[7], rsem, section=mate).wait_recv()

    pending, drains = [], []

    def go(copy, when=None):
        if when is None:
            copy.start()
        else:
            pl.when(when)(copy.start)
        pending.append((copy, when))

    barrier = pltpu.get_barrier_semaphore()
    friends = [(mod(sec + k, LAYERS), dp) for k in range(1, LAYERS)]
    friends += [(sec, at_dp(z, mod(y + k, NY))) for k in range(1, NY)]
    friends += [(sec, at_dp(mod(z + k, NZ), y)) for k in range(1, NZ)]
    for section, replica in friends:
        pl.semaphore_signal(
            barrier, inc=1, device_id={"section": section, "dp": replica}, device_id_type=MESH
        )
    pl.semaphore_wait(barrier, len(friends))

    w_home = lax.div(z, 2)
    w_zl = lax.rem(z, 2)
    w_away = w_home != x
    w_place = wall.at[c, x, w_zl * NY + y]
    w_local = pltpu.make_async_copy(w_hbm, w_place, s_loc.at[0])
    x_load = pltpu.make_async_copy(x_hbm, xv, s_loc.at[1])
    q_load = pltpu.make_async_copy(q_hbm, qv, s_loc.at[2])
    half = D // LAYERS

    def rows(b):
        return pl.ds(pl.multiple_of(b * SEQ, 16), SEQ)

    def top_half(b):
        return top.at[:, pl.ds(aligned(b, half), half)]

    og_local = pltpu.make_async_copy(og_hbm.at[rows(c)], top_half(c), s_loc.at[3])

    def dest(k):
        section = mod(sec + k, LAYERS)
        return section, lax.div(section, 2), lax.rem(section, 2)

    def block(ref, b, g):
        return ref.at[rows(b), pl.ds(aligned(g, GROUP), GROUP)]

    xi_local = pltpu.make_async_copy(block(x_hbm, c, x), xi.at[sec], s_loc.at[4])

    def send_weights():
        used = sec != 0
        for h in range(2):
            part = pl.ds(h * CUT, CUT)
            go(
                send(
                    w_hbm.at[part], w_place.at[part], s_wx.at[h], r_w.at[x, w_zl, h],
                    section=2 * w_home + c,
                ),
                jnp.logical_and(used, w_away),
            )
        pl.when(jnp.logical_and(used, jnp.logical_not(w_away)))(w_local.start)

    def send_inputs():
        for i in range(D // BLK):
            gain_ref[i:i + 1, :] = gain_bf[:, i * BLK:(i + 1) * BLK].astype(F32)
        q_load.start()
        x_load.start()
        go(send(og_hbm.at[rows(1 - c)], top_half(c), s_og, r_og, section=mate))
        og_local.start()
        for k in range(1, LAYERS):
            section, g, b = dest(k)
            go(send(block(x_hbm, b, g), xi.at[sec], s_x.at[k], r_x.at[sec], section=section))
            gain = gain_ref.at[pl.ds(aligned(g, 8), 8)]
            go(send(gain, gain_in.at[sec], s_g.at[k], r_g.at[sec], section=section))
        xi_local.start()
        gain_in[sec] = gain_ref[pl.ds(aligned(x, 8), 8)]

    def probabilities(g, b):
        keys = k_ref[rows(b), pl.ds(aligned(g, HD), HD)]
        stacked = jnp.concatenate(
            [
                qv[rows(b), pl.ds(pl.multiple_of(g * GROUP + h * HD, HD), HD)]
                for h in range(PER)
            ],
            axis=0,
        )
        scores = lax.dot_general(keys, stacked, NT, preferred_element_type=F32)
        scores = scores * HD ** (-0.5) + mask[...]
        exponent = jnp.exp(scores - jnp.max(scores, axis=0, keepdims=True))
        return (exponent / jnp.sum(exponent, axis=0, keepdims=True)).astype(BF16)

    def p_copy(k):
        section, g, b = dest(k)
        return send(p_own.at[k], pt.at[sec], s_p.at[k], r_p.at[sec], section=section)

    def send_probabilities():
        key_row = lax.broadcasted_iota(jnp.int32, (SEQ, STACK), 0)
        query_row = lax.rem(lax.broadcasted_iota(jnp.int32, (SEQ, STACK), 1), SEQ)
        mask[...] = jnp.where(key_row <= query_row, 0.0, -1e30).astype(F32)
        q_load.wait()

        @pl.loop(1, LAYERS)
        def _(k):
            section, g, b = dest(k)
            p_own[k] = probabilities(g, b)
            p_copy(k).start()

        pt[sec] = probabilities(x, c)

        def drain():
            @pl.loop(1, LAYERS)
            def _(k):
                p_copy(k).wait_send()

        drains.append(drain)

    def send_inverse():
        x_load.wait()

        def squares(i, acc):
            v = xv[:, pl.ds(aligned(i, HD), HD)].astype(F32)
            return acc + v * v

        acc = lax.fori_loop(0, D // HD, squares, jnp.zeros((2 * SEQ, HD), F32))
        mean = jnp.sum(acc, axis=1, keepdims=True) * (1.0 / D)
        inv_own[...] = jnp.broadcast_to(lax.rsqrt(mean + EPSILON), (2 * SEQ, HD))
        for k in range(1, LAYERS):
            section, g, b = dest(k)
            go(send(inv_own.at[rows(b)], inv_in.at[sec], s_i.at[k], r_i.at[sec], section=section))
        inv_in[sec] = inv_own[rows(c)]

    def make_hidden():
        @pl.loop(0, D // BLK)
        def _(i):
            cols = pl.ds(aligned(i, BLK), BLK)
            normed = xv[:, cols].astype(F32) * inv_own[:, 0:1]
            h_own[lax.rem(i, NY), :, pl.ds(aligned(lax.div(i, NY), BLK), BLK)] = (
                normed * gain_ref[pl.ds(i, 1), :]
            ).astype(BF16)

    d = mod(2 * x - z, NZ)
    downward = d <= 3
    step = jnp.where(downward, -1, 1)
    first = jnp.where(downward, 0, 1)
    source = jnp.logical_or(d == 0, d == 7)
    onward = jnp.logical_and(d != 3, d != 4)
    z_out, z_in = mod(z + step, NZ), mod(z - step, NZ)
    y_right, y_left, y_far = mod(y + 1, NY), mod(y - 1, NY), mod(y + 2, NY)

    def piece_ref(u, piece, yy, h):
        return wall.at[c, u, piece * NY + yy, pl.ds(h * CUT, CUT)]

    def live(u, cond=None):
        if u > 0:
            return cond
        return c == 1 if cond is None else jnp.logical_and(c == 1, cond)

    def arrived_if(cond, dst, rsem):
        if cond is None:
            arrived(dst, rsem)
        else:
            pl.when(cond)(lambda: arrived(dst, rsem))

    def column(u):
        for o in range(2):
            piece = first if o == 0 else 1 - first
            if o == 0:
                mine = jnp.logical_and(source, x == u)
                pl.when(live(u, mine))(w_local.wait)
            for h in range(2):
                ref = piece_ref(u, piece, y, h)
                sem = r_w.at[u, piece, h]
                if o == 0:
                    arrived_if(live(u, jnp.logical_not(mine)), ref, sem)
                    inward = send(ref, ref, s_z.at[u, 2, h], sem, replica=at_dp(z_in, y))
                    go(inward, live(u, source))
                else:
                    arrived_if(live(u), ref, sem)
                outward = send(ref, ref, s_z.at[u, o, h], sem, replica=at_dp(z_out, y))
                go(outward, live(u, onward))
                for i, yy in enumerate((y_right, y_left)):
                    sems = s_y.at[u, o, i, h], r_y.at[u, piece, y, h]
                    go(send(ref, ref, *sems, replica=at_dp(z, yy)), live(u))

    def near(u, piece, yy, h):
        arrived_if(live(u), piece_ref(u, piece, yy, h), r_y.at[u, piece, yy, h])

    def row(u):
        for h in range(2):
            for piece, source_y, to_y in ((0, y_left, y_right), (1, y_right, y_left)):
                near(u, piece, source_y, h)
                ref = piece_ref(u, piece, source_y, h)
                sems = s_yf.at[u, piece, h], r_y.at[u, piece, source_y, h]
                go(send(ref, ref, *sems, replica=at_dp(z, to_y)), live(u))

    def finish(u):
        for h in range(2):
            near(u, 1, y_left, h)
            near(u, 0, y_right, h)
        for h in range(2):
            for piece in range(2):
                near(u, piece, y_far, h)
        go(send(wall.at[c, u], wall.at[c, u], s_pt.at[u], r_pt.at[u], section=mate), live(u))

    def weights_ready(u):
        cond = None if u > 0 else c == 0
        arrived_if(cond, wall.at[1 - c, u], r_pt.at[u])

    def h_rows(yy):
        return h_all.at[pl.ds(aligned(yy, 2 * SEQ), 2 * SEQ)]

    def send_hidden():
        for k in range(1, NY):
            yy = mod(y + k, NY)
            go(send(h_own.at[yy], h_rows(y), s_h.at[k], r_h.at[y], replica=at_dp(z, yy)))
        h_all[pl.ds(aligned(y, 2 * SEQ), 2 * SEQ), :] = h_own[y]

    def hidden_ready():
        for k in range(1, NY):
            yy = mod(y + k, NY)
            arrived(h_rows(yy), r_h.at[yy])

    def top_ready():
        og_local.wait()
        arrived(top_half(1 - c), r_og)
        for h in range(PER):
            up[h * SEQ:(h + 1) * SEQ, :] = top[:, h * HD:(h + 1) * HD]

    def inputs_ready(s):
        pl.when(s == sec)(xi_local.wait)

        @pl.when(s != sec)
        def _():
            arrived(xi.at[s], r_x.at[s])
            arrived(pt.at[s], r_p.at[s])
            arrived(inv_in.at[s], r_i.at[s])
            arrived(gain_in.at[s], r_g.at[s])

    def peers():
        return [mod(x + k, NX) for k in range(1, NX)]

    def w_block(s, i):
        return wall[s % 2, s // 2, i]

    def v_part(s, k):
        g = mod(x + k, NX)
        return send(
            v_own.at[s, g], v_in.at[s, x], s_v.at[s, k], r_v.at[s, x], section=2 * g + c
        )

    def v_start(s):
        inverse = inv_in[s][:, 0:1]
        acc = jnp.zeros((SEQ, KV), F32)
        for i in range(GROUP // BLK):
            cols = slice(i * BLK, (i + 1) * BLK)
            normed = xi[s, :, cols].astype(F32) * inverse
            hidden = (normed * gain_in[s, i:i + 1, :]).astype(BF16)
            acc += jnp.dot(hidden, w_block(s, i), preferred_element_type=F32)
        for g in range(NX):
            v_own[s, g] = acc[:, g * HD:(g + 1) * HD].astype(BF16)
        for k in range(1, NX):
            v_part(s, k).start()

    def v_cols(s, g):
        return v_all.at[s, :, pl.ds(aligned(g, HD), HD)]

    def v_sum_copy(s, k):
        g = mod(x + k, NX)
        return send(v_cols(s, x), v_cols(s, x), s_w.at[s, k], r_vs.at[s, x], section=2 * g + c)

    def v_sum(s):
        acc = v_own[s, x].astype(F32)
        for g in peers():
            arrived(v_in.at[s, g], r_v.at[s, g])
            acc += v_in[s, g].astype(F32)
        v_all[s, :, pl.ds(aligned(x, HD), HD)] = acc.astype(BF16)
        for k in range(1, NX):
            v_sum_copy(s, k).start()

    def v_ready(s):
        for g in peers():
            arrived(v_cols(s, g), r_vs.at[s, g])

    def vg_cols(s, g):
        return vgb.at[s, :, pl.ds(aligned(g, HD), HD)]

    def vg_copies(s):
        return [
            send(vg_cols(s, x), vg_cols(s, x), s_vg.at[s, k], r_vg.at[s, x], section=2 * g + c)
            for k, g in enumerate(peers())
        ]

    def vg_place(b):
        return pl.ds(pl.multiple_of(y * 2 * SEQ + b * SEQ, 16), SEQ)

    def vp_copy(s):
        return send(vgb.at[s], vg_all.at[vg_place(c)], s_vp, r_vp, section=mate)

    def vg_start(s):
        grad = jnp.dot(pt[s], up[...], preferred_element_type=F32).astype(BF16)
        vgb[s, :, pl.ds(aligned(x, HD), HD)] = grad
        for copy in vg_copies(s):
            copy.start()

    def vg_ready(s):
        for g in peers():
            arrived(vg_cols(s, g), r_vg.at[s, g])
        pl.when(mate == s)(lambda: vp_copy(s).start())

    def update(s):
        grads = vgb[s]
        inner = grads.astype(F32) * v_all[s].astype(F32)
        inner = jnp.sum(inner, axis=1, keepdims=True) * (1.0 / D)
        inverse = inv_in[s][:, 0:1]
        for i in range(GROUP // BLK):
            cols = slice(i * BLK, (i + 1) * BLK)
            hidden_grad = lax.dot_general(grads, w_block(s, i), NT, preferred_element_type=F32)
            normed = xi[s, :, cols].astype(F32) * inverse
            change = inverse * (hidden_grad * gain_in[s, i:i + 1, :] - normed * inner)
            for j in range(BLK // HD):
                h = i * (BLK // HD) + j
                place = slice(h * SEQ, (h + 1) * SEQ)
                up[place, :] = (
                    up[place, :].astype(F32) + change[:, j * HD:(j + 1) * HD]
                ).astype(BF16)

    def update_last(s):
        grads = vgb[s]
        inverse = inv_in[s][:, 0:1]
        partial = jnp.zeros((SEQ, HD), F32)
        for i in range(GROUP // BLK):
            cols = slice(i * BLK, (i + 1) * BLK)
            hidden_grad = lax.dot_general(grads, w_block(s, i), NT, preferred_element_type=F32)
            scaled = hidden_grad * gain_in[s, i:i + 1, :]
            hg[:, cols] = scaled
            product = scaled * (xi[s, :, cols].astype(F32) * inverse)
            partial += product[:, :HD] + product[:, HD:]
        partial = jnp.sum(partial, axis=1, keepdims=True)
        inner_in[x] = jnp.broadcast_to(partial, (SEQ, HD))
        for k in range(1, NX):
            g = mod(x + k, NX)
            go(
                send(
                    inner_in.at[x], inner_in.at[x], s_in.at[k], r_in.at[x], section=2 * g + c
                )
            )
        for g in peers():
            arrived(inner_in.at[g], r_in.at[g])
        inner = sum(inner_in[g] for g in range(NX))[:, 0:1] * (1.0 / D)
        for h in range(PER):
            cols = slice(h * HD, (h + 1) * HD)
            place = slice(h * SEQ, (h + 1) * SEQ)
            change = inverse * (hg[:, cols] - xi[s, :, cols].astype(F32) * inverse * inner)
            up[place, :] = (up[place, :].astype(F32) + change).astype(BF16)

    def drain_chain():
        @pl.loop(0, LAYERS)
        def _(s):
            for copy in vg_copies(s):
                copy.wait_send()

        @pl.loop(2, LAYERS)
        def _(s):
            for k in range(1, NX):
                v_part(s, k).wait_send()
                v_sum_copy(s, k).wait_send()

        vp_copy(mate).wait_send()

    def vg_rows(yy):
        return vg_all.at[pl.ds(aligned(yy, 2 * SEQ), 2 * SEQ)]

    def send_value_grads():
        vg_all[vg_place(c)] = vgb[sec]
        arrived(vg_all.at[vg_place(1 - c)], r_vp)
        for k in range(1, NY):
            yy = mod(y + k, NY)
            go(send(vg_rows(y), vg_rows(y), s_vy.at[k], r_vy.at[y], replica=at_dp(z, yy)))
        for k in range(1, NY):
            yy = mod(y + k, NY)
            arrived(vg_rows(yy), r_vy.at[yy])

    def product(q, owner):
        return jnp.dot(
            vg_t[q * CUT:(q + 1) * CUT, :], h_all[:, pl.ds(aligned(owner, BLK), BLK)],
            preferred_element_type=F32,
        )

    def rs_copy(way, m, q):
        to = mod(z + 1, NZ) if way == 0 else mod(z - 1, NZ)
        return send(
            rs_send.at[way, m, q], rs_recv.at[way, m, q], s_rs.at[way, m, q],
            r_rs.at[way, m, q], replica=at_dp(to, y),
        )

    def pass_on(way, m, q, joined):
        ahead = HOPS - m
        part = product(q, mod(z + ahead, NZ) if way == 0 else mod(z - ahead, NZ))
        if joined:
            rs_copy(way, m - 1, q).wait_recv()
            part += rs_recv[way, m - 1, q].astype(F32)
        rs_send[way, m, q] = part.astype(BF16)
        go(rs_copy(way, m, q))

    def reduce_products():
        vg_t[...] = vg_all[...].astype(F32).T.astype(BF16)
        far = ((0, 1), (2, 3))
        rest = ((2, 3), (0, 1))
        for i in range(2):
            for way in range(2):
                pass_on(way, 0, far[way][i], False)
        for i in range(2):
            for way in range(2):
                pass_on(way, 1, rest[way][i], False)
        for i in range(2):
            for way in range(2):
                pass_on(way, 1, far[way][i], True)
        for m in range(2, HOPS):
            for group in (rest, far):
                for i in range(2):
                    for way in range(2):
                        pass_on(way, m, group[way][i], True)
        squares_sum = jnp.zeros((1, 1), F32)
        for q in range(STREAMS):
            total[q] = product(q, z)
        for q in (2, 0, 3, 1):
            owned = total[q]
            for way in range(2):
                rs_copy(way, HOPS - 1, q).wait_recv()
                owned += rs_recv[way, HOPS - 1, q].astype(F32)
            total[q] = owned
            part = jnp.sum(owned * owned, axis=1, keepdims=True)
            squares_sum += jnp.sum(part, axis=0, keepdims=True)
        return squares_sum

    def clip(squares_sum):
        stages = (
            (n1, LAYERS, sec, lambda i: (i, dp)),
            (n2, NY, y, lambda i: (sec, at_dp(z, i))),
            (n3, NZ, z, lambda i: (sec, at_dp(i, y))),
        )
        value = jnp.broadcast_to(squares_sum, (8, 128))
        for t, (slots, count, me, place) in enumerate(stages):
            slots[me] = value
            for k in range(1, count):
                section, replica = place(mod(me + k, count))
                go(
                    send(
                        slots.at[me], slots.at[me], s_n.at[t, k], r_n.at[t, me], section=section,
                        replica=replica,
                    )
                )
            for k in range(1, count):
                i = mod(me + k, count)
                arrived(slots.at[i], r_n.at[t, i])
            value = sum(slots[i] for i in range(count))
        ceiling = float(LAYERS * D * KV) ** 0.5
        factor = jnp.minimum(1.0, ceiling / jnp.sqrt(value[0:1, 0:1]))
        for q in range(STREAMS):
            out_ref[:, q * CUT:(q + 1) * CUT] = (total[q] * factor).T

    send_weights()
    send_inputs()
    send_inverse()
    send_probabilities()
    column(3)
    make_hidden()
    column(2)
    row(3)
    finish(3)
    column(1)
    top_ready()
    inputs_ready(7)
    inputs_ready(6)
    weights_ready(3)
    v_start(7)
    v_start(6)
    row(2)
    column(0)
    v_sum(7)
    vg_start(7)
    v_sum(6)
    finish(2)
    v_ready(7)
    vg_ready(7)
    update(7)
    vg_start(6)
    row(1)
    v_ready(6)
    vg_ready(6)
    update(6)
    inputs_ready(5)
    inputs_ready(4)
    weights_ready(2)
    v_start(5)
    v_start(4)
    finish(1)
    row(0)
    send_hidden()
    v_sum(5)
    vg_start(5)
    v_sum(4)
    v_ready(5)
    vg_ready(5)
    update(5)
    vg_start(4)
    finish(0)
    v_ready(4)
    vg_ready(4)
    update(4)
    inputs_ready(3)
    inputs_ready(2)
    inputs_ready(1)
    inputs_ready(0)
    weights_ready(1)
    v_start(3)
    v_start(2)
    v_sum(3)
    vg_start(3)
    v_sum(2)
    v_ready(3)
    vg_ready(3)
    update(3)
    vg_start(2)
    v_ready(2)
    vg_ready(2)
    update(2)
    vg_start(1)
    vg_ready(1)
    weights_ready(0)
    update_last(1)
    vg_start(0)
    vg_ready(0)
    drains.append(drain_chain)
    send_value_grads()
    hidden_ready()
    clip(reduce_products())

    for drain in drains:
        drain()
    for copy, when in pending:
        if when is None:
            copy.wait_send()
        else:
            pl.when(when)(copy.wait_send)


def shards(layer_inputs, queries, keys, gains, value_weights, out_grad):
    dma, vmem = pltpu.SemaphoreType.DMA, pltpu.VMEM
    scratch = [
        vmem((D // BLK, BLK), F32),
        vmem((2 * SEQ, D), BF16),
        vmem((2 * SEQ, D), BF16),
        vmem((2, NX, 2 * NY, BLK, KV), BF16),
        vmem((LAYERS, SEQ, GROUP), BF16),
        vmem((LAYERS, SEQ, STACK), BF16),
        vmem((LAYERS, SEQ, HD), F32),
        vmem((LAYERS, 8, BLK), F32),
        vmem((LAYERS, SEQ, STACK), BF16),
        vmem((2 * SEQ, HD), F32),
        vmem((SEQ, STACK), F32),
        vmem((SEQ, GROUP), BF16),
        vmem((STACK, HD), BF16),
        vmem((LAYERS, SEQ, KV), BF16),
        vmem((LAYERS, NX, SEQ, HD), BF16),
        vmem((LAYERS, NX, SEQ, HD), BF16),
        vmem((LAYERS, SEQ, KV), BF16),
        vmem((SEQ, GROUP), F32),
        vmem((NX, SEQ, HD), F32),
        vmem((NY, 2 * SEQ, GROUP), BF16),
        vmem((NY * 2 * SEQ, GROUP), BF16),
        vmem((NY * 2 * SEQ, KV), BF16),
        vmem((KV, NY * 2 * SEQ), BF16),
        vmem((2, HOPS, STREAMS, CUT, BLK), BF16),
        vmem((2, HOPS, STREAMS, CUT, BLK), BF16),
        vmem((STREAMS, CUT, BLK), F32),
        vmem((LAYERS, 8, 128), F32),
        vmem((NY, 8, 128), F32),
        vmem((NZ, 8, 128), F32),
        dma((8,)),
        dma((LAYERS,)), dma((LAYERS,)),
        dma((LAYERS,)), dma((LAYERS,)),
        dma((LAYERS,)), dma((LAYERS,)),
        dma((LAYERS,)), dma((LAYERS,)),
        dma, dma,
        dma((2,)), dma((NX, 2, 2)), dma((NX, 3, 2)), dma((NX, 2, 2, 2)), dma((NX, 2, 2)),
        dma((NX, 2, NY, 2)),
        dma((NX,)), dma((NX,)),
        dma((LAYERS, NX)), dma((LAYERS, NX)), dma((LAYERS, NX)), dma((LAYERS, NX)),
        dma((NX,)), dma((NX,)),
        dma((LAYERS, NX)), dma((LAYERS, NX)),
        dma, dma,
        dma((NY,)), dma((NY,)),
        dma((NY,)), dma((NY,)),
        dma((2, HOPS, STREAMS)), dma((2, HOPS, STREAMS)),
        dma((3, LAYERS)), dma((3, LAYERS)),
    ]
    hbm, whole = pl.BlockSpec(memory_space=pl.ANY), pl.BlockSpec(memory_space=pltpu.VMEM)
    out = pl.pallas_call(
        body,
        out_shape=jax.ShapeDtypeStruct((BLK, KV), F32),
        in_specs=[hbm, hbm, whole, whole, hbm, hbm],
        out_specs=whole,
        scratch_shapes=scratch,
        compiler_params=pltpu.CompilerParams(
            collective_id=0, has_side_effects=True, vmem_limit_bytes=60 * 1024 * 1024
        ),
    )(layer_inputs[0], queries[0], keys[0], gains, value_weights[0], out_grad)
    return out[None]


def solution(mesh):
    return jax.shard_map(
        shards,
        mesh=mesh,
        in_specs=(
            P("section", "dp", None),
            P("section", "dp", None),
            P("section", "dp", None),
            P("section", None),
            P("section", "dp", None),
            P("dp", "section"),
        ),
        out_specs=P("section", "dp", None),
        check_vma=False,
    )
```

```python
import jax
import jax.numpy as jnp
from jax import lax
from jax.experimental import pallas as pl
from jax.experimental.pallas import tpu as pltpu
from jax.sharding import PartitionSpec as P

MESH = pl.DeviceIdType.MESH
F32, BF16 = jnp.float32, jnp.bfloat16
QH, KVH, HD, SEQ, D = 64, 4, 128, 80, 8192
PER = QH // KVH
GROUP = PER * HD
KV = KVH * HD
STACK = PER * SEQ
BLK = 256
CUT = 128
HOPS = 4
STREAMS = KV // CUT
LAYERS, NX, NY, NZ = 8, 4, 4, 8
EPSILON = 1e-05
NT = (((1,), (1,)), ((), ()))


def mod(a, n):
    return lax.rem(a + 2 * n, n)


def aligned(index, size):
    return pl.multiple_of(index * size, size)


def body(
    x_hbm, q_hbm, k_ref, gain_bf, w_hbm, og_hbm, out_ref, gain_ref,
    xv, qv, wall, xi, pt, inv_in, gain_in, p_own, inv_own, mask, top, up, vgb, v_own, v_in, v_all, hg, inner_in,
    h_own, h_all, vg_all, vg_t, rs_send, rs_recv, total, n1, n2, n3,
    s_loc, s_x, r_x, s_p, r_p, s_i, r_i, s_g, r_g, s_og, r_og, s_wx, r_w, s_z, s_y, s_yf, r_y,
    s_pt, r_pt, s_v, r_v, s_w, r_vs, s_in, r_in, s_vg, r_vg, s_vy, r_vy, s_h, r_h, s_rs, r_rs, s_n, r_n,
):
    sec, dp = lax.axis_index("section"), lax.axis_index("dp")
    x, c = lax.div(sec, 2), lax.rem(sec, 2)
    z, y = lax.div(dp, NY), lax.rem(dp, NY)
    mate = sec + 1 - 2 * c

    def at_dp(zz, yy):
        return zz * NY + yy

    def send(src, dst, ssem, rsem, section=sec, replica=dp):
        return pltpu.make_async_remote_copy(
            src_ref=src, dst_ref=dst, send_sem=ssem, recv_sem=rsem,
            device_id={"section": section, "dp": replica}, device_id_type=MESH,
        )

    def arrived(dst, rsem):
        send(dst, dst, s_loc.at[7], rsem, section=mate).wait_recv()

    pending, drains = [], []

    def go(copy, when=None):
        if when is None:
            copy.start()
        else:
            pl.when(when)(copy.start)
        pending.append((copy, when))

    barrier = pltpu.get_barrier_semaphore()
    friends = [(mod(sec + k, LAYERS), dp) for k in range(1, LAYERS)]
    friends += [(sec, at_dp(z, mod(y + k, NY))) for k in range(1, NY)]
    friends += [(mate, at_dp(z, mod(y + k, NY))) for k in range(1, NY)]
    friends += [(sec, at_dp(mod(z + k, NZ), y)) for k in range(1, NZ)]
    for section, replica in friends:
        pl.semaphore_signal(
            barrier, inc=1, device_id={"section": section, "dp": replica}, device_id_type=MESH
        )
    pl.semaphore_wait(barrier, len(friends))

    w_home = lax.div(z, 2)
    w_zl = lax.rem(z, 2)
    w_away = w_home != x
    w_place = wall.at[c, x, w_zl * NY + y]
    w_local = pltpu.make_async_copy(w_hbm, w_place, s_loc.at[0])
    x_load = pltpu.make_async_copy(x_hbm, xv, s_loc.at[1])
    q_load = pltpu.make_async_copy(q_hbm, qv, s_loc.at[2])
    half = D // LAYERS

    def rows(b):
        return pl.ds(pl.multiple_of(b * SEQ, 16), SEQ)

    def top_half(b):
        return top.at[:, pl.ds(aligned(b, half), half)]

    og_local = pltpu.make_async_copy(og_hbm.at[rows(c)], top_half(c), s_loc.at[3])

    def dest(k):
        section = mod(sec + k, LAYERS)
        return section, lax.div(section, 2), lax.rem(section, 2)

    def block(ref, b, g):
        return ref.at[rows(b), pl.ds(aligned(g, GROUP), GROUP)]

    xi_local = pltpu.make_async_copy(block(x_hbm, c, x), xi.at[sec], s_loc.at[4])

    def send_weights():
        used = sec != 0
        for h in range(2):
            part = pl.ds(h * CUT, CUT)
            go(
                send(
                    w_hbm.at[part], w_place.at[part], s_wx.at[h], r_w.at[x, w_zl, h],
                    section=2 * w_home + c,
                ),
                jnp.logical_and(used, w_away),
            )
        pl.when(jnp.logical_and(used, jnp.logical_not(w_away)))(w_local.start)

    def x_copy(k):
        section, g, b = dest(k)
        return send(block(x_hbm, b, g), xi.at[sec], s_x.at[k], r_x.at[sec], section=section)

    def send_inputs():
        for i in range(D // BLK):
            gain_ref[i:i + 1, :] = gain_bf[:, i * BLK:(i + 1) * BLK].astype(F32)
        q_load.start()
        x_load.start()
        go(send(og_hbm.at[rows(1 - c)], top_half(c), s_og, r_og, section=mate))
        og_local.start()
        for k in range(1, LAYERS):
            section, g, b = dest(k)
            go(x_copy(k), sec > 0)
            gain = gain_ref.at[pl.ds(aligned(g, 8), 8)]
            go(send(gain, gain_in.at[sec], s_g.at[k], r_g.at[sec], section=section), sec > 0)
        xi_local.start()
        gain_in[sec] = gain_ref[pl.ds(aligned(x, 8), 8)]

    def probabilities(g, b):
        keys = k_ref[rows(b), pl.ds(aligned(g, HD), HD)]
        stacked = jnp.concatenate(
            [
                qv[rows(b), pl.ds(pl.multiple_of(g * GROUP + h * HD, HD), HD)]
                for h in range(PER)
            ],
            axis=0,
        )
        scores = lax.dot_general(keys, stacked, NT, preferred_element_type=F32)
        scores = scores * HD ** (-0.5) + mask[...]
        exponent = jnp.exp(scores - jnp.max(scores, axis=0, keepdims=True))
        return (exponent / jnp.sum(exponent, axis=0, keepdims=True)).astype(BF16)

    def p_copy(k):
        section, g, b = dest(k)
        return send(p_own.at[k], pt.at[sec], s_p.at[k], r_p.at[sec], section=section)

    def send_probabilities():
        key_row = lax.broadcasted_iota(jnp.int32, (SEQ, STACK), 0)
        query_row = lax.rem(lax.broadcasted_iota(jnp.int32, (SEQ, STACK), 1), SEQ)
        mask[...] = jnp.where(key_row <= query_row, 0.0, -1e30).astype(F32)
        q_load.wait()

        @pl.loop(1, LAYERS)
        def _(k):
            section, g, b = dest(k)
            p_own[k] = probabilities(g, b)
            p_copy(k).start()

        pt[sec] = probabilities(x, c)

        def drain():
            @pl.loop(1, LAYERS)
            def _(k):
                p_copy(k).wait_send()

        drains.append(drain)

    def send_inverse():
        x_load.wait()

        def squares(i, acc):
            v = xv[:, pl.ds(aligned(i, HD), HD)].astype(F32)
            return acc + v * v

        acc = lax.fori_loop(0, D // HD, squares, jnp.zeros((2 * SEQ, HD), F32))
        mean = jnp.sum(acc, axis=1, keepdims=True) * (1.0 / D)
        inv_own[...] = jnp.broadcast_to(lax.rsqrt(mean + EPSILON), (2 * SEQ, HD))
        for k in range(1, LAYERS):
            section, g, b = dest(k)
            copy = send(
                inv_own.at[rows(b)], inv_in.at[sec], s_i.at[k], r_i.at[sec], section=section
            )
            go(copy, sec > 0)
        inv_in[sec] = inv_own[rows(c)]

    def make_hidden():
        @pl.loop(0, D // BLK)
        def _(i):
            cols = pl.ds(aligned(i, BLK), BLK)
            normed = xv[:, cols].astype(F32) * inv_own[:, 0:1]
            h_own[lax.rem(i, NY), :, pl.ds(aligned(lax.div(i, NY), BLK), BLK)] = (
                normed * gain_ref[pl.ds(i, 1), :]
            ).astype(BF16)

    d = mod(2 * x - z, NZ)
    downward = d <= 3
    step = jnp.where(downward, -1, 1)
    first = jnp.where(downward, 0, 1)
    source = jnp.logical_or(d == 0, d == 7)
    onward = jnp.logical_and(d != 3, d != 4)
    z_out, z_in = mod(z + step, NZ), mod(z - step, NZ)
    y_right, y_left, y_far = mod(y + 1, NY), mod(y - 1, NY), mod(y + 2, NY)

    def piece_ref(u, piece, yy, h):
        return wall.at[c, u, piece * NY + yy, pl.ds(h * CUT, CUT)]

    def live(u, cond=None):
        if u > 0:
            return cond
        return c == 1 if cond is None else jnp.logical_and(c == 1, cond)

    def arrived_if(cond, dst, rsem):
        if cond is None:
            arrived(dst, rsem)
        else:
            pl.when(cond)(lambda: arrived(dst, rsem))

    def column(u):
        for o in range(2):
            piece = first if o == 0 else 1 - first
            if o == 0:
                mine = jnp.logical_and(source, x == u)
                pl.when(live(u, mine))(w_local.wait)
            for h in range(2):
                ref = piece_ref(u, piece, y, h)
                sem = r_w.at[u, piece, h]
                if o == 0:
                    arrived_if(live(u, jnp.logical_not(mine)), ref, sem)
                    inward = send(ref, ref, s_z.at[u, 2, h], sem, replica=at_dp(z_in, y))
                    go(inward, live(u, source))
                else:
                    arrived_if(live(u), ref, sem)
                outward = send(ref, ref, s_z.at[u, o, h], sem, replica=at_dp(z_out, y))
                go(outward, live(u, onward))
                for i, yy in enumerate((y_right, y_left)):
                    sems = s_y.at[u, o, i, h], r_y.at[u, piece, y, h]
                    go(send(ref, ref, *sems, replica=at_dp(z, yy)), live(u))

    def near(u, piece, yy, h):
        arrived_if(live(u), piece_ref(u, piece, yy, h), r_y.at[u, piece, yy, h])

    def row(u):
        for h in range(2):
            for piece, source_y, to_y in ((0, y_left, y_right), (1, y_right, y_left)):
                near(u, piece, source_y, h)
                ref = piece_ref(u, piece, source_y, h)
                sems = s_yf.at[u, piece, h], r_y.at[u, piece, source_y, h]
                go(send(ref, ref, *sems, replica=at_dp(z, to_y)), live(u))

    def finish(u):
        for h in range(2):
            near(u, 1, y_left, h)
            near(u, 0, y_right, h)
        for h in range(2):
            for piece in range(2):
                near(u, piece, y_far, h)
        go(send(wall.at[c, u], wall.at[c, u], s_pt.at[u], r_pt.at[u], section=mate), live(u))

    def weights_ready(u):
        cond = None if u > 0 else c == 0
        arrived_if(cond, wall.at[1 - c, u], r_pt.at[u])

    def h_rows(yy):
        return h_all.at[pl.ds(aligned(yy, 2 * SEQ), 2 * SEQ)]

    def send_hidden():
        for k in range(1, NY):
            yy = mod(y + k, NY)
            go(send(h_own.at[yy], h_rows(y), s_h.at[k], r_h.at[y], replica=at_dp(z, yy)))
        h_all[pl.ds(aligned(y, 2 * SEQ), 2 * SEQ), :] = h_own[y]

    def hidden_ready():
        for k in range(1, NY):
            yy = mod(y + k, NY)
            arrived(h_rows(yy), r_h.at[yy])

    def top_ready():
        og_local.wait()
        arrived(top_half(1 - c), r_og)
        for h in range(PER):
            up[h * SEQ:(h + 1) * SEQ, :] = top[:, h * HD:(h + 1) * HD]

    def inputs_ready(s):
        pl.when(s == sec)(xi_local.wait)

        @pl.when(s != sec)
        def _():
            arrived(pt.at[s], r_p.at[s])
            if s > 0:
                arrived(xi.at[s], r_x.at[s])
                arrived(inv_in.at[s], r_i.at[s])
                arrived(gain_in.at[s], r_g.at[s])

    def peers():
        return [mod(x + k, NX) for k in range(1, NX)]

    def w_block(s, i):
        return wall[s % 2, s // 2, i]

    def v_part(s, k):
        g = mod(x + k, NX)
        return send(
            v_own.at[s, g], v_in.at[s, x], s_v.at[s, k], r_v.at[s, x], section=2 * g + c
        )

    def v_start(s):
        inverse = inv_in[s][:, 0:1]
        acc = jnp.zeros((SEQ, KV), F32)
        for i in range(GROUP // BLK):
            cols = slice(i * BLK, (i + 1) * BLK)
            normed = xi[s, :, cols].astype(F32) * inverse
            hidden = (normed * gain_in[s, i:i + 1, :]).astype(BF16)
            acc += jnp.dot(hidden, w_block(s, i), preferred_element_type=F32)
        for g in range(NX):
            v_own[s, g] = acc[:, g * HD:(g + 1) * HD].astype(BF16)
        for k in range(1, NX):
            v_part(s, k).start()

    def v_cols(s, g):
        return v_all.at[s, :, pl.ds(aligned(g, HD), HD)]

    def v_sum_copy(s, k):
        g = mod(x + k, NX)
        return send(v_cols(s, x), v_cols(s, x), s_w.at[s, k], r_vs.at[s, x], section=2 * g + c)

    def v_sum(s):
        acc = v_own[s, x].astype(F32)
        for g in peers():
            arrived(v_in.at[s, g], r_v.at[s, g])
            acc += v_in[s, g].astype(F32)
        v_all[s, :, pl.ds(aligned(x, HD), HD)] = acc.astype(BF16)
        for k in range(1, NX):
            v_sum_copy(s, k).start()

    def v_ready(s):
        for g in peers():
            arrived(v_cols(s, g), r_vs.at[s, g])

    def vg_cols(s, g):
        return vgb.at[s, :, pl.ds(aligned(g, HD), HD)]

    def vg_copies(s):
        return [
            send(vg_cols(s, x), vg_cols(s, x), s_vg.at[s, k], r_vg.at[s, x], section=2 * g + c)
            for k, g in enumerate(peers())
        ]

    def vg_place(b):
        return pl.ds(pl.multiple_of(y * 2 * SEQ + b * SEQ, 16), SEQ)

    def vy_copy(s, k):
        rows_here = vg_all.at[vg_place(c)]
        return send(
            vgb.at[s], rows_here, s_vy.at[s % 2, k], r_vy.at[y, c], section=s,
            replica=at_dp(z, mod(y + k, NY)),
        )

    def vg_start(s):
        grad = jnp.dot(pt[s], up[...], preferred_element_type=F32).astype(BF16)
        vgb[s, :, pl.ds(aligned(x, HD), HD)] = grad
        for copy in vg_copies(s):
            copy.start()

    def vg_ready(s):
        for g in peers():
            arrived(vg_cols(s, g), r_vg.at[s, g])

        @pl.when(x == s // 2)
        def _():
            for k in range(1, NY):
                vy_copy(s, k).start()

        pl.when(mate == s)(lambda: vy_copy(s, 0).start())

    def update(s):
        grads = vgb[s]
        inner = grads.astype(F32) * v_all[s].astype(F32)
        inner = jnp.sum(inner, axis=1, keepdims=True) * (1.0 / D)
        inverse = inv_in[s][:, 0:1]
        for i in range(GROUP // BLK):
            cols = slice(i * BLK, (i + 1) * BLK)
            hidden_grad = lax.dot_general(grads, w_block(s, i), NT, preferred_element_type=F32)
            normed = xi[s, :, cols].astype(F32) * inverse
            change = inverse * (hidden_grad * gain_in[s, i:i + 1, :] - normed * inner)
            for j in range(BLK // HD):
                h = i * (BLK // HD) + j
                place = slice(h * SEQ, (h + 1) * SEQ)
                up[place, :] = (
                    up[place, :].astype(F32) + change[:, j * HD:(j + 1) * HD]
                ).astype(BF16)

    def update_last(s):
        grads = vgb[s]
        inverse = inv_in[s][:, 0:1]
        partial = jnp.zeros((SEQ, HD), F32)
        for i in range(GROUP // BLK):
            cols = slice(i * BLK, (i + 1) * BLK)
            hidden_grad = lax.dot_general(grads, w_block(s, i), NT, preferred_element_type=F32)
            scaled = hidden_grad * gain_in[s, i:i + 1, :]
            hg[:, cols] = scaled
            product = scaled * (xi[s, :, cols].astype(F32) * inverse)
            partial += product[:, :HD] + product[:, HD:]
        partial = jnp.sum(partial, axis=1, keepdims=True)
        inner_in[x] = jnp.broadcast_to(partial, (SEQ, HD))
        for k in range(1, NX):
            g = mod(x + k, NX)
            go(
                send(
                    inner_in.at[x], inner_in.at[x], s_in.at[k], r_in.at[x], section=2 * g + c
                )
            )
        for g in peers():
            arrived(inner_in.at[g], r_in.at[g])
        inner = sum(inner_in[g] for g in range(NX))[:, 0:1] * (1.0 / D)
        for h in range(PER):
            cols = slice(h * HD, (h + 1) * HD)
            place = slice(h * SEQ, (h + 1) * SEQ)
            change = inverse * (hg[:, cols] - xi[s, :, cols].astype(F32) * inverse * inner)
            up[place, :] = (up[place, :].astype(F32) + change).astype(BF16)

    def drain_chain():
        @pl.loop(0, LAYERS)
        def _(s):
            for copy in vg_copies(s):
                copy.wait_send()

        @pl.loop(2, LAYERS)
        def _(s):
            for k in range(1, NX):
                v_part(s, k).wait_send()
                v_sum_copy(s, k).wait_send()

        for k in range(1, NY):
            vy_copy(sec, k).wait_send()
            vy_copy(mate, k).wait_send()
        vy_copy(mate, 0).wait_send()

    def value_grads_ready():
        vg_all[vg_place(c)] = vgb[sec]
        for k in range(NY):
            yy = mod(y + k, NY)
            for b in (1 - c,) if k == 0 else (0, 1):
                place = pl.ds(pl.multiple_of(yy * 2 * SEQ + b * SEQ, 16), SEQ)
                arrived(vg_all.at[place], r_vy.at[yy, b])

    def product(q, owner):
        return jnp.dot(
            vg_t[q * CUT:(q + 1) * CUT, :], h_all[:, pl.ds(aligned(owner, BLK), BLK)],
            preferred_element_type=F32,
        )

    def rs_copy(way, m, q):
        to = mod(z + 1, NZ) if way == 0 else mod(z - 1, NZ)
        return send(
            rs_send.at[way, m, q], rs_recv.at[way, m, q], s_rs.at[way, m, q],
            r_rs.at[way, m, q], replica=at_dp(to, y),
        )

    def pass_on(way, m, q, joined):
        ahead = HOPS - m
        part = product(q, mod(z + ahead, NZ) if way == 0 else mod(z - ahead, NZ))
        if joined:
            rs_copy(way, m - 1, q).wait_recv()
            part += rs_recv[way, m - 1, q].astype(F32)
        rs_send[way, m, q] = part.astype(BF16)
        go(rs_copy(way, m, q))

    def reduce_products():
        vg_t[...] = vg_all[...].astype(F32).T.astype(BF16)
        far = ((0, 1), (2, 3))
        rest = ((2, 3), (0, 1))
        for i in range(2):
            for way in range(2):
                pass_on(way, 0, far[way][i], False)
        for i in range(2):
            for way in range(2):
                pass_on(way, 1, rest[way][i], False)
        for i in range(2):
            for way in range(2):
                pass_on(way, 1, far[way][i], True)
        for m in range(2, HOPS):
            for group in (rest, far):
                for i in range(2):
                    for way in range(2):
                        pass_on(way, m, group[way][i], True)
        squares_sum = jnp.zeros((1, 1), F32)
        for q in range(STREAMS):
            total[q] = product(q, z)
        for q in (2, 0, 3, 1):
            owned = total[q]
            for way in range(2):
                rs_copy(way, HOPS - 1, q).wait_recv()
                owned += rs_recv[way, HOPS - 1, q].astype(F32)
            total[q] = owned
            part = jnp.sum(owned * owned, axis=1, keepdims=True)
            squares_sum += jnp.sum(part, axis=0, keepdims=True)
        return squares_sum

    def clip(squares_sum):
        stages = (
            (n1, LAYERS, sec, lambda i: (i, dp)),
            (n2, NY, y, lambda i: (sec, at_dp(z, i))),
            (n3, NZ, z, lambda i: (sec, at_dp(i, y))),
        )
        value = jnp.broadcast_to(squares_sum, (8, 128))
        for t, (slots, count, me, place) in enumerate(stages):
            slots[me] = value
            for k in range(1, count):
                section, replica = place(mod(me + k, count))
                go(
                    send(
                        slots.at[me], slots.at[me], s_n.at[t, k], r_n.at[t, me], section=section,
                        replica=replica,
                    )
                )
            for k in range(1, count):
                i = mod(me + k, count)
                arrived(slots.at[i], r_n.at[t, i])
            value = sum(slots[i] for i in range(count))
        ceiling = float(LAYERS * D * KV) ** 0.5
        factor = jnp.minimum(1.0, ceiling / jnp.sqrt(value[0:1, 0:1]))
        for q in range(STREAMS):
            out_ref[:, q * CUT:(q + 1) * CUT] = (total[q] * factor).T

    send_weights()
    send_inputs()
    send_inverse()
    send_probabilities()
    column(3)
    make_hidden()
    column(2)
    row(3)
    finish(3)
    column(1)
    top_ready()
    inputs_ready(7)
    inputs_ready(6)
    vg_start(7)
    weights_ready(3)
    v_start(7)
    v_start(6)
    row(2)
    column(0)
    v_sum(7)
    v_sum(6)
    finish(2)
    v_ready(7)
    vg_ready(7)
    update(7)
    vg_start(6)
    row(1)
    v_ready(6)
    vg_ready(6)
    update(6)
    inputs_ready(5)
    inputs_ready(4)
    vg_start(5)
    weights_ready(2)
    v_start(5)
    v_start(4)
    finish(1)
    row(0)
    send_hidden()
    v_sum(5)
    v_sum(4)
    v_ready(5)
    vg_ready(5)
    update(5)
    vg_start(4)
    finish(0)
    v_ready(4)
    vg_ready(4)
    update(4)
    inputs_ready(3)
    inputs_ready(2)
    inputs_ready(1)
    inputs_ready(0)
    vg_start(3)
    weights_ready(1)
    v_start(3)
    v_start(2)
    v_sum(3)
    v_sum(2)
    v_ready(3)
    vg_ready(3)
    update(3)
    vg_start(2)
    v_ready(2)
    vg_ready(2)
    update(2)
    vg_start(1)
    vg_ready(1)
    weights_ready(0)
    update_last(1)
    vg_start(0)
    vg_ready(0)
    drains.append(drain_chain)
    value_grads_ready()
    hidden_ready()
    clip(reduce_products())

    for drain in drains:
        drain()
    for copy, when in pending:
        if when is None:
            copy.wait_send()
        else:
            pl.when(when)(copy.wait_send)


def shards(layer_inputs, queries, keys, gains, value_weights, out_grad):
    dma, vmem = pltpu.SemaphoreType.DMA, pltpu.VMEM
    scratch = [
        vmem((D // BLK, BLK), F32),
        vmem((2 * SEQ, D), BF16),
        vmem((2 * SEQ, D), BF16),
        vmem((2, NX, 2 * NY, BLK, KV), BF16),
        vmem((LAYERS, SEQ, GROUP), BF16),
        vmem((LAYERS, SEQ, STACK), BF16),
        vmem((LAYERS, SEQ, HD), F32),
        vmem((LAYERS, 8, BLK), F32),
        vmem((LAYERS, SEQ, STACK), BF16),
        vmem((2 * SEQ, HD), F32),
        vmem((SEQ, STACK), F32),
        vmem((SEQ, GROUP), BF16),
        vmem((STACK, HD), BF16),
        vmem((LAYERS, SEQ, KV), BF16),
        vmem((LAYERS, NX, SEQ, HD), BF16),
        vmem((LAYERS, NX, SEQ, HD), BF16),
        vmem((LAYERS, SEQ, KV), BF16),
        vmem((SEQ, GROUP), F32),
        vmem((NX, SEQ, HD), F32),
        vmem((NY, 2 * SEQ, GROUP), BF16),
        vmem((NY * 2 * SEQ, GROUP), BF16),
        vmem((NY * 2 * SEQ, KV), BF16),
        vmem((KV, NY * 2 * SEQ), BF16),
        vmem((2, HOPS, STREAMS, CUT, BLK), BF16),
        vmem((2, HOPS, STREAMS, CUT, BLK), BF16),
        vmem((STREAMS, CUT, BLK), F32),
        vmem((LAYERS, 8, 128), F32),
        vmem((NY, 8, 128), F32),
        vmem((NZ, 8, 128), F32),
        dma((8,)),
        dma((LAYERS,)), dma((LAYERS,)),
        dma((LAYERS,)), dma((LAYERS,)),
        dma((LAYERS,)), dma((LAYERS,)),
        dma((LAYERS,)), dma((LAYERS,)),
        dma, dma,
        dma((2,)), dma((NX, 2, 2)), dma((NX, 3, 2)), dma((NX, 2, 2, 2)), dma((NX, 2, 2)),
        dma((NX, 2, NY, 2)),
        dma((NX,)), dma((NX,)),
        dma((LAYERS, NX)), dma((LAYERS, NX)), dma((LAYERS, NX)), dma((LAYERS, NX)),
        dma((NX,)), dma((NX,)),
        dma((LAYERS, NX)), dma((LAYERS, NX)),
        dma((2, NY)), dma((NY, 2)),
        dma((NY,)), dma((NY,)),
        dma((2, HOPS, STREAMS)), dma((2, HOPS, STREAMS)),
        dma((3, LAYERS)), dma((3, LAYERS)),
    ]
    hbm, whole = pl.BlockSpec(memory_space=pl.ANY), pl.BlockSpec(memory_space=pltpu.VMEM)
    out = pl.pallas_call(
        body,
        out_shape=jax.ShapeDtypeStruct((BLK, KV), F32),
        in_specs=[hbm, hbm, whole, whole, hbm, hbm],
        out_specs=whole,
        scratch_shapes=scratch,
        compiler_params=pltpu.CompilerParams(
            collective_id=0, has_side_effects=True, vmem_limit_bytes=60 * 1024 * 1024
        ),
    )(layer_inputs[0], queries[0], keys[0], gains, value_weights[0], out_grad)
    return out[None]


def solution(mesh):
    return jax.shard_map(
        shards,
        mesh=mesh,
        in_specs=(
            P("section", "dp", None),
            P("section", "dp", None),
            P("section", "dp", None),
            P("section", None),
            P("section", "dp", None),
            P("dp", "section"),
        ),
        out_specs=P("section", "dp", None),
        check_vma=False,
    )
```

```python
import jax
import jax.numpy as jnp
from jax import lax
from jax.experimental import pallas as pl
from jax.experimental.pallas import tpu as pltpu
from jax.sharding import PartitionSpec as P

MESH = pl.DeviceIdType.MESH
F32, BF16 = jnp.float32, jnp.bfloat16
QH, KVH, HD, SEQ, D = 64, 4, 128, 80, 8192
PER = QH // KVH
GROUP = PER * HD
KV = KVH * HD
STACK = PER * SEQ
BLK = 256
CUT = 128
HOPS = 4
STREAMS = KV // CUT
LAYERS, NX, NY, NZ = 8, 4, 4, 8
EPSILON = 1e-05
NT = (((1,), (1,)), ((), ()))


def mod(a, n):
    return lax.rem(a + 2 * n, n)


def aligned(index, size):
    return pl.multiple_of(index * size, size)


def body(
    x_hbm, q_hbm, k_ref, gain_bf, w_hbm, og_hbm, out_ref, gain_ref,
    xv, qv, wall, xi, pt, inv_in, gain_in, p_own, inv_own, mask, top, up, vgb, v_own, v_in, v_all, hg, inner_in,
    h_own, h_all, vg_all, vg_t, rs_send, rs_recv, total, n1, n3,
    s_loc, s_x, r_x, s_p, r_p, s_i, r_i, s_g, r_g, s_og, r_og, s_wx, r_w, s_z, s_y, s_yf, r_y,
    s_pt, r_pt, s_v, r_v, s_w, r_vs, s_in, r_in, s_vg, r_vg, s_vy, r_vy, s_h, r_h, s_rs, r_rs, s_n, r_n,
):
    sec, dp = lax.axis_index("section"), lax.axis_index("dp")
    x, c = lax.div(sec, 2), lax.rem(sec, 2)
    z, y = lax.div(dp, NY), lax.rem(dp, NY)
    mate = sec + 1 - 2 * c

    def at_dp(zz, yy):
        return zz * NY + yy

    def send(src, dst, ssem, rsem, section=sec, replica=dp):
        return pltpu.make_async_remote_copy(
            src_ref=src, dst_ref=dst, send_sem=ssem, recv_sem=rsem,
            device_id={"section": section, "dp": replica}, device_id_type=MESH,
        )

    def arrived(dst, rsem):
        send(dst, dst, s_loc.at[7], rsem, section=mate).wait_recv()

    pending, drains = [], []

    def go(copy, when=None):
        if when is None:
            copy.start()
        else:
            pl.when(when)(copy.start)
        pending.append((copy, when))

    barrier = pltpu.get_barrier_semaphore()
    friends = [(mod(sec + k, LAYERS), dp) for k in range(1, LAYERS)]
    friends += [(sec, at_dp(z, mod(y + k, NY))) for k in range(1, NY)]
    for i in range(1, LAYERS):
        friends += [(mod(sec + i, LAYERS), at_dp(z, mod(y + k, NY))) for k in range(1, NY)]
    friends += [(sec, at_dp(mod(z + k, NZ), y)) for k in range(1, NZ)]
    for section, replica in friends:
        pl.semaphore_signal(
            barrier, inc=1, device_id={"section": section, "dp": replica}, device_id_type=MESH
        )
    pl.semaphore_wait(barrier, len(friends))

    w_home = lax.div(z, 2)
    w_zl = lax.rem(z, 2)
    w_away = w_home != x
    w_place = wall.at[c, x, w_zl * NY + y]
    w_local = pltpu.make_async_copy(w_hbm, w_place, s_loc.at[0])
    x_load = pltpu.make_async_copy(x_hbm, xv, s_loc.at[1])
    q_load = pltpu.make_async_copy(q_hbm, qv, s_loc.at[2])
    half = D // LAYERS

    def rows(b):
        return pl.ds(pl.multiple_of(b * SEQ, 16), SEQ)

    def top_half(b):
        return top.at[:, pl.ds(aligned(b, half), half)]

    og_local = pltpu.make_async_copy(og_hbm.at[rows(c)], top_half(c), s_loc.at[3])

    def dest(k):
        section = mod(sec + k, LAYERS)
        return section, lax.div(section, 2), lax.rem(section, 2)

    def block(ref, b, g):
        return ref.at[rows(b), pl.ds(aligned(g, GROUP), GROUP)]

    xi_local = pltpu.make_async_copy(block(x_hbm, c, x), xi.at[sec], s_loc.at[4])

    def send_weights():
        used = sec != 0
        for h in range(2):
            part = pl.ds(h * CUT, CUT)
            go(
                send(
                    w_hbm.at[part], w_place.at[part], s_wx.at[h], r_w.at[x, w_zl, h],
                    section=2 * w_home + c,
                ),
                jnp.logical_and(used, w_away),
            )
        pl.when(jnp.logical_and(used, jnp.logical_not(w_away)))(w_local.start)

    def x_copy(k):
        section, g, b = dest(k)
        return send(block(x_hbm, b, g), xi.at[sec], s_x.at[k], r_x.at[sec], section=section)

    def send_inputs():
        for i in range(D // BLK):
            gain_ref[i:i + 1, :] = gain_bf[:, i * BLK:(i + 1) * BLK].astype(F32)
        q_load.start()
        x_load.start()
        go(send(og_hbm.at[rows(1 - c)], top_half(c), s_og, r_og, section=mate))
        og_local.start()
        for k in range(1, LAYERS):
            section, g, b = dest(k)
            go(x_copy(k), sec > 0)
            gain = gain_ref.at[pl.ds(aligned(g, 8), 8)]
            go(send(gain, gain_in.at[sec], s_g.at[k], r_g.at[sec], section=section), sec > 0)
        xi_local.start()
        gain_in[sec] = gain_ref[pl.ds(aligned(x, 8), 8)]

    def probabilities(g, b):
        keys = k_ref[rows(b), pl.ds(aligned(g, HD), HD)]
        stacked = jnp.concatenate(
            [
                qv[rows(b), pl.ds(pl.multiple_of(g * GROUP + h * HD, HD), HD)]
                for h in range(PER)
            ],
            axis=0,
        )
        scores = lax.dot_general(keys, stacked, NT, preferred_element_type=F32)
        scores = scores * HD ** (-0.5) + mask[...]
        exponent = jnp.exp(scores - jnp.max(scores, axis=0, keepdims=True))
        return (exponent / jnp.sum(exponent, axis=0, keepdims=True)).astype(BF16)

    def p_copy(k):
        section, g, b = dest(k)
        return send(p_own.at[k], pt.at[sec], s_p.at[k], r_p.at[sec], section=section)

    def send_probabilities():
        key_row = lax.broadcasted_iota(jnp.int32, (SEQ, STACK), 0)
        query_row = lax.rem(lax.broadcasted_iota(jnp.int32, (SEQ, STACK), 1), SEQ)
        mask[...] = jnp.where(key_row <= query_row, 0.0, -1e30).astype(F32)
        q_load.wait()

        @pl.loop(1, LAYERS)
        def _(k):
            section, g, b = dest(k)
            p_own[k] = probabilities(g, b)
            p_copy(k).start()

        pt[sec] = probabilities(x, c)

        def drain():
            @pl.loop(1, LAYERS)
            def _(k):
                p_copy(k).wait_send()

        drains.append(drain)

    def send_inverse():
        x_load.wait()

        def squares(i, acc):
            v = xv[:, pl.ds(aligned(i, HD), HD)].astype(F32)
            return acc + v * v

        acc = lax.fori_loop(0, D // HD, squares, jnp.zeros((2 * SEQ, HD), F32))
        mean = jnp.sum(acc, axis=1, keepdims=True) * (1.0 / D)
        inv_own[...] = jnp.broadcast_to(lax.rsqrt(mean + EPSILON), (2 * SEQ, HD))
        for k in range(1, LAYERS):
            section, g, b = dest(k)
            copy = send(
                inv_own.at[rows(b)], inv_in.at[sec], s_i.at[k], r_i.at[sec], section=section
            )
            go(copy, sec > 0)
        inv_in[sec] = inv_own[rows(c)]

    def make_hidden():
        @pl.loop(0, D // BLK)
        def _(i):
            cols = pl.ds(aligned(i, BLK), BLK)
            normed = xv[:, cols].astype(F32) * inv_own[:, 0:1]
            h_own[lax.rem(i, NY), :, pl.ds(aligned(lax.div(i, NY), BLK), BLK)] = (
                normed * gain_ref[pl.ds(i, 1), :]
            ).astype(BF16)

    d = mod(2 * x - z, NZ)
    downward = d <= 3
    step = jnp.where(downward, -1, 1)
    first = jnp.where(downward, 0, 1)
    source = jnp.logical_or(d == 0, d == 7)
    onward = jnp.logical_and(d != 3, d != 4)
    z_out, z_in = mod(z + step, NZ), mod(z - step, NZ)
    y_right, y_left, y_far = mod(y + 1, NY), mod(y - 1, NY), mod(y + 2, NY)

    def piece_ref(u, piece, yy, h):
        return wall.at[c, u, piece * NY + yy, pl.ds(h * CUT, CUT)]

    def live(u, cond=None):
        if u > 0:
            return cond
        return c == 1 if cond is None else jnp.logical_and(c == 1, cond)

    def arrived_if(cond, dst, rsem):
        if cond is None:
            arrived(dst, rsem)
        else:
            pl.when(cond)(lambda: arrived(dst, rsem))

    def column(u):
        for o in range(2):
            piece = first if o == 0 else 1 - first
            if o == 0:
                mine = jnp.logical_and(source, x == u)
                pl.when(live(u, mine))(w_local.wait)
            for h in range(2):
                ref = piece_ref(u, piece, y, h)
                sem = r_w.at[u, piece, h]
                if o == 0:
                    arrived_if(live(u, jnp.logical_not(mine)), ref, sem)
                    inward = send(ref, ref, s_z.at[u, 2, h], sem, replica=at_dp(z_in, y))
                    go(inward, live(u, source))
                else:
                    arrived_if(live(u), ref, sem)
                outward = send(ref, ref, s_z.at[u, o, h], sem, replica=at_dp(z_out, y))
                go(outward, live(u, onward))
                for i, yy in enumerate((y_right, y_left)):
                    sems = s_y.at[u, o, i, h], r_y.at[u, piece, y, h]
                    go(send(ref, ref, *sems, replica=at_dp(z, yy)), live(u))

    def near(u, piece, yy, h):
        arrived_if(live(u), piece_ref(u, piece, yy, h), r_y.at[u, piece, yy, h])

    def row(u):
        for h in range(2):
            for piece, source_y, to_y in ((0, y_left, y_right), (1, y_right, y_left)):
                near(u, piece, source_y, h)
                ref = piece_ref(u, piece, source_y, h)
                sems = s_yf.at[u, piece, h], r_y.at[u, piece, source_y, h]
                go(send(ref, ref, *sems, replica=at_dp(z, to_y)), live(u))

    def finish(u):
        for h in range(2):
            near(u, 1, y_left, h)
            near(u, 0, y_right, h)
        for h in range(2):
            for piece in range(2):
                near(u, piece, y_far, h)
        go(send(wall.at[c, u], wall.at[c, u], s_pt.at[u], r_pt.at[u], section=mate), live(u))

    def weights_ready(u):
        cond = None if u > 0 else c == 0
        arrived_if(cond, wall.at[1 - c, u], r_pt.at[u])

    def h_rows(yy):
        return h_all.at[pl.ds(aligned(yy, 2 * SEQ), 2 * SEQ)]

    def send_hidden():
        for k in range(1, NY):
            yy = mod(y + k, NY)
            go(send(h_own.at[yy], h_rows(y), s_h.at[k], r_h.at[y], replica=at_dp(z, yy)))
        h_all[pl.ds(aligned(y, 2 * SEQ), 2 * SEQ), :] = h_own[y]

    def hidden_ready():
        for k in range(1, NY):
            yy = mod(y + k, NY)
            arrived(h_rows(yy), r_h.at[yy])

    def top_ready():
        og_local.wait()
        arrived(top_half(1 - c), r_og)
        for h in range(PER):
            up[h * SEQ:(h + 1) * SEQ, :] = top[:, h * HD:(h + 1) * HD]

    def inputs_ready(s):
        pl.when(s == sec)(xi_local.wait)

        @pl.when(s != sec)
        def _():
            arrived(pt.at[s], r_p.at[s])
            if s > 0:
                arrived(xi.at[s], r_x.at[s])
                arrived(inv_in.at[s], r_i.at[s])
                arrived(gain_in.at[s], r_g.at[s])

    def peers():
        return [mod(x + k, NX) for k in range(1, NX)]

    def w_block(s, i):
        return wall[s % 2, s // 2, i]

    def v_part(s, k):
        g = mod(x + k, NX)
        return send(
            v_own.at[s, g], v_in.at[s, x], s_v.at[s, k], r_v.at[s, x], section=2 * g + c
        )

    def v_start(s):
        inverse = inv_in[s][:, 0:1]
        acc = jnp.zeros((SEQ, KV), F32)
        for i in range(GROUP // BLK):
            cols = slice(i * BLK, (i + 1) * BLK)
            normed = xi[s, :, cols].astype(F32) * inverse
            hidden = (normed * gain_in[s, i:i + 1, :]).astype(BF16)
            acc += jnp.dot(hidden, w_block(s, i), preferred_element_type=F32)
        for g in range(NX):
            v_own[s, g] = acc[:, g * HD:(g + 1) * HD].astype(BF16)
        for k in range(1, NX):
            v_part(s, k).start()

    def v_cols(s, g):
        return v_all.at[s, :, pl.ds(aligned(g, HD), HD)]

    def v_sum_copy(s, k):
        g = mod(x + k, NX)
        return send(v_cols(s, x), v_cols(s, x), s_w.at[s, k], r_vs.at[s, x], section=2 * g + c)

    def v_sum(s):
        acc = v_own[s, x].astype(F32)
        for g in peers():
            arrived(v_in.at[s, g], r_v.at[s, g])
            acc += v_in[s, g].astype(F32)
        v_all[s, :, pl.ds(aligned(x, HD), HD)] = acc.astype(BF16)
        for k in range(1, NX):
            v_sum_copy(s, k).start()

    def v_ready(s):
        for g in peers():
            arrived(v_cols(s, g), r_vs.at[s, g])

    def vg_cols(s, g):
        return vgb.at[s, :, pl.ds(aligned(g, HD), HD)]

    def vg_copies(s):
        return [
            send(vg_cols(s, x), vg_cols(s, x), s_vg.at[s, k], r_vg.at[s, x], section=2 * g + c)
            for k, g in enumerate(peers())
        ]

    def vg_place(b):
        return pl.ds(pl.multiple_of(y * 2 * SEQ + b * SEQ, 16), SEQ)

    def vy_copy(s, k):
        rows_here = vg_all.at[vg_place(c)]
        return send(
            vgb.at[s], rows_here, s_vy.at[s % 2, k], r_vy.at[y, c], section=s,
            replica=at_dp(z, mod(y + k, NY)),
        )

    def vg_start(s):
        grad = jnp.dot(pt[s], up[...], preferred_element_type=F32).astype(BF16)
        vgb[s, :, pl.ds(aligned(x, HD), HD)] = grad
        for copy in vg_copies(s):
            copy.start()

    def vg_ready(s):
        for g in peers():
            arrived(vg_cols(s, g), r_vg.at[s, g])

        @pl.when(x == s // 2)
        def _():
            for k in range(1, NY):
                vy_copy(s, k).start()

        pl.when(mate == s)(lambda: vy_copy(s, 0).start())

    def update(s):
        grads = vgb[s]
        inner = grads.astype(F32) * v_all[s].astype(F32)
        inner = jnp.sum(inner, axis=1, keepdims=True) * (1.0 / D)
        inverse = inv_in[s][:, 0:1]
        for i in range(GROUP // BLK):
            cols = slice(i * BLK, (i + 1) * BLK)
            hidden_grad = lax.dot_general(grads, w_block(s, i), NT, preferred_element_type=F32)
            normed = xi[s, :, cols].astype(F32) * inverse
            change = inverse * (hidden_grad * gain_in[s, i:i + 1, :] - normed * inner)
            for j in range(BLK // HD):
                h = i * (BLK // HD) + j
                place = slice(h * SEQ, (h + 1) * SEQ)
                up[place, :] = (
                    up[place, :].astype(F32) + change[:, j * HD:(j + 1) * HD]
                ).astype(BF16)

    def update_last(s):
        grads = vgb[s]
        inverse = inv_in[s][:, 0:1]
        partial = jnp.zeros((SEQ, HD), F32)
        for i in range(GROUP // BLK):
            cols = slice(i * BLK, (i + 1) * BLK)
            hidden_grad = lax.dot_general(grads, w_block(s, i), NT, preferred_element_type=F32)
            scaled = hidden_grad * gain_in[s, i:i + 1, :]
            hg[:, cols] = scaled
            product = scaled * (xi[s, :, cols].astype(F32) * inverse)
            partial += product[:, :HD] + product[:, HD:]
        partial = jnp.sum(partial, axis=1, keepdims=True)
        inner_in[x] = jnp.broadcast_to(partial, (SEQ, HD))
        for k in range(1, NX):
            g = mod(x + k, NX)
            go(
                send(
                    inner_in.at[x], inner_in.at[x], s_in.at[k], r_in.at[x], section=2 * g + c
                )
            )
        for g in peers():
            arrived(inner_in.at[g], r_in.at[g])
        inner = sum(inner_in[g] for g in range(NX))[:, 0:1] * (1.0 / D)
        for h in range(PER):
            cols = slice(h * HD, (h + 1) * HD)
            place = slice(h * SEQ, (h + 1) * SEQ)
            change = inverse * (hg[:, cols] - xi[s, :, cols].astype(F32) * inverse * inner)
            up[place, :] = (up[place, :].astype(F32) + change).astype(BF16)

    def drain_chain():
        @pl.loop(0, LAYERS)
        def _(s):
            for copy in vg_copies(s):
                copy.wait_send()

        @pl.loop(2, LAYERS)
        def _(s):
            for k in range(1, NX):
                v_part(s, k).wait_send()
                v_sum_copy(s, k).wait_send()

        for k in range(1, NY):
            vy_copy(sec, k).wait_send()
            vy_copy(mate, k).wait_send()
        vy_copy(mate, 0).wait_send()

    def value_grads_ready():
        vg_all[vg_place(c)] = vgb[sec]
        for k in range(NY):
            yy = mod(y + k, NY)
            for b in (1 - c,) if k == 0 else (0, 1):
                place = pl.ds(pl.multiple_of(yy * 2 * SEQ + b * SEQ, 16), SEQ)
                arrived(vg_all.at[place], r_vy.at[yy, b])

    def product(q, owner):
        return jnp.dot(
            vg_t[q * CUT:(q + 1) * CUT, :], h_all[:, pl.ds(aligned(owner, BLK), BLK)],
            preferred_element_type=F32,
        )

    def rs_copy(way, m, q):
        to = mod(z + 1, NZ) if way == 0 else mod(z - 1, NZ)
        return send(
            rs_send.at[way, m, q], rs_recv.at[way, m, q], s_rs.at[way, m, q],
            r_rs.at[way, m, q], replica=at_dp(to, y),
        )

    def pass_on(way, m, q, joined):
        ahead = HOPS - m
        part = product(q, mod(z + ahead, NZ) if way == 0 else mod(z - ahead, NZ))
        if joined:
            rs_copy(way, m - 1, q).wait_recv()
            part += rs_recv[way, m - 1, q].astype(F32)
        rs_send[way, m, q] = part.astype(BF16)
        go(rs_copy(way, m, q))

    def reduce_products():
        vg_t[...] = vg_all[...].astype(F32).T.astype(BF16)
        far = ((0, 1), (2, 3))
        rest = ((2, 3), (0, 1))
        for i in range(2):
            for way in range(2):
                pass_on(way, 0, far[way][i], False)
        for i in range(2):
            for way in range(2):
                pass_on(way, 1, rest[way][i], False)
        for i in range(2):
            for way in range(2):
                pass_on(way, 1, far[way][i], True)
        for m in range(2, HOPS):
            for group in (rest, far):
                for i in range(2):
                    for way in range(2):
                        pass_on(way, m, group[way][i], True)
        squares_sum = jnp.zeros((1, 1), F32)
        for q in range(STREAMS):
            total[q] = product(q, z)
        for q in (2, 0, 3, 1):
            owned = total[q]
            for way in range(2):
                rs_copy(way, HOPS - 1, q).wait_recv()
                owned += rs_recv[way, HOPS - 1, q].astype(F32)
            total[q] = owned
            part = jnp.sum(owned * owned, axis=1, keepdims=True)
            squares_sum += jnp.sum(part, axis=0, keepdims=True)
        return squares_sum

    def clip(squares_sum):
        stages = (
            (n1, LAYERS * NY, sec * NY + y, lambda i: (lax.div(i, NY), at_dp(z, lax.rem(i, NY)))),
            (n3, NZ, z, lambda i: (sec, at_dp(i, y))),
        )
        value = jnp.broadcast_to(squares_sum, (8, 128))
        for t, (slots, count, me, place) in enumerate(stages):
            slots[me] = value
            for k in range(1, count):
                section, replica = place(mod(me + k, count))
                go(
                    send(
                        slots.at[me], slots.at[me], s_n.at[t, k], r_n.at[t, me], section=section,
                        replica=replica,
                    )
                )
            for k in range(1, count):
                i = mod(me + k, count)
                arrived(slots.at[i], r_n.at[t, i])
            value = sum(slots[i] for i in range(count))
        ceiling = float(LAYERS * D * KV) ** 0.5
        factor = jnp.minimum(1.0, ceiling / jnp.sqrt(value[0:1, 0:1]))
        for q in range(STREAMS):
            out_ref[:, q * CUT:(q + 1) * CUT] = (total[q] * factor).T

    send_weights()
    send_inputs()
    send_inverse()
    send_probabilities()
    column(3)
    make_hidden()
    column(2)
    row(3)
    finish(3)
    column(1)
    top_ready()
    inputs_ready(7)
    inputs_ready(6)
    vg_start(7)
    weights_ready(3)
    v_start(7)
    v_start(6)
    row(2)
    column(0)
    v_sum(7)
    v_sum(6)
    finish(2)
    v_ready(7)
    vg_ready(7)
    update(7)
    vg_start(6)
    row(1)
    v_ready(6)
    vg_ready(6)
    update(6)
    inputs_ready(5)
    inputs_ready(4)
    vg_start(5)
    weights_ready(2)
    v_start(5)
    v_start(4)
    finish(1)
    row(0)
    send_hidden()
    v_sum(5)
    v_sum(4)
    v_ready(5)
    vg_ready(5)
    update(5)
    vg_start(4)
    finish(0)
    v_ready(4)
    vg_ready(4)
    update(4)
    inputs_ready(3)
    inputs_ready(2)
    inputs_ready(1)
    inputs_ready(0)
    vg_start(3)
    weights_ready(1)
    v_start(3)
    v_start(2)
    v_sum(3)
    v_sum(2)
    v_ready(3)
    vg_ready(3)
    update(3)
    vg_start(2)
    v_ready(2)
    vg_ready(2)
    update(2)
    vg_start(1)
    vg_ready(1)
    weights_ready(0)
    update_last(1)
    vg_start(0)
    vg_ready(0)
    drains.append(drain_chain)
    value_grads_ready()
    hidden_ready()
    clip(reduce_products())

    for drain in drains:
        drain()
    for copy, when in pending:
        if when is None:
            copy.wait_send()
        else:
            pl.when(when)(copy.wait_send)


def shards(layer_inputs, queries, keys, gains, value_weights, out_grad):
    dma, vmem = pltpu.SemaphoreType.DMA, pltpu.VMEM
    scratch = [
        vmem((D // BLK, BLK), F32),
        vmem((2 * SEQ, D), BF16),
        vmem((2 * SEQ, D), BF16),
        vmem((2, NX, 2 * NY, BLK, KV), BF16),
        vmem((LAYERS, SEQ, GROUP), BF16),
        vmem((LAYERS, SEQ, STACK), BF16),
        vmem((LAYERS, SEQ, HD), F32),
        vmem((LAYERS, 8, BLK), F32),
        vmem((LAYERS, SEQ, STACK), BF16),
        vmem((2 * SEQ, HD), F32),
        vmem((SEQ, STACK), F32),
        vmem((SEQ, GROUP), BF16),
        vmem((STACK, HD), BF16),
        vmem((LAYERS, SEQ, KV), BF16),
        vmem((LAYERS, NX, SEQ, HD), BF16),
        vmem((LAYERS, NX, SEQ, HD), BF16),
        vmem((LAYERS, SEQ, KV), BF16),
        vmem((SEQ, GROUP), F32),
        vmem((NX, SEQ, HD), F32),
        vmem((NY, 2 * SEQ, GROUP), BF16),
        vmem((NY * 2 * SEQ, GROUP), BF16),
        vmem((NY * 2 * SEQ, KV), BF16),
        vmem((KV, NY * 2 * SEQ), BF16),
        vmem((2, HOPS, STREAMS, CUT, BLK), BF16),
        vmem((2, HOPS, STREAMS, CUT, BLK), BF16),
        vmem((STREAMS, CUT, BLK), F32),
        vmem((LAYERS * NY, 8, 128), F32),
        vmem((NZ, 8, 128), F32),
        dma((8,)),
        dma((LAYERS,)), dma((LAYERS,)),
        dma((LAYERS,)), dma((LAYERS,)),
        dma((LAYERS,)), dma((LAYERS,)),
        dma((LAYERS,)), dma((LAYERS,)),
        dma, dma,
        dma((2,)), dma((NX, 2, 2)), dma((NX, 3, 2)), dma((NX, 2, 2, 2)), dma((NX, 2, 2)),
        dma((NX, 2, NY, 2)),
        dma((NX,)), dma((NX,)),
        dma((LAYERS, NX)), dma((LAYERS, NX)), dma((LAYERS, NX)), dma((LAYERS, NX)),
        dma((NX,)), dma((NX,)),
        dma((LAYERS, NX)), dma((LAYERS, NX)),
        dma((2, NY)), dma((NY, 2)),
        dma((NY,)), dma((NY,)),
        dma((2, HOPS, STREAMS)), dma((2, HOPS, STREAMS)),
        dma((2, LAYERS * NY)), dma((2, LAYERS * NY)),
    ]
    hbm, whole = pl.BlockSpec(memory_space=pl.ANY), pl.BlockSpec(memory_space=pltpu.VMEM)
    out = pl.pallas_call(
        body,
        out_shape=jax.ShapeDtypeStruct((BLK, KV), F32),
        in_specs=[hbm, hbm, whole, whole, hbm, hbm],
        out_specs=whole,
        scratch_shapes=scratch,
        compiler_params=pltpu.CompilerParams(
            collective_id=0, has_side_effects=True, vmem_limit_bytes=60 * 1024 * 1024
        ),
    )(layer_inputs[0], queries[0], keys[0], gains, value_weights[0], out_grad)
    return out[None]


def solution(mesh):
    return jax.shard_map(
        shards,
        mesh=mesh,
        in_specs=(
            P("section", "dp", None),
            P("section", "dp", None),
            P("section", "dp", None),
            P("section", None),
            P("section", "dp", None),
            P("dp", "section"),
        ),
        out_specs=P("section", "dp", None),
        check_vma=False,
    )
```
